32 devices in a mesh: stream: 2 (over x), wide: 16 (over z, y, core).
Axes of the slice: x: 2, y: 2, z: 4, core: 2. Of those that a mesh axis runs over, the one named last changes fastest.
Arguments:
- tokens: bfloat16 [2, 16, 512, 768], P('stream', 'wide'), may hold values from -6 to 6
- doc_segments: int32 [16, 512], P('wide'), may hold values from 0 to 3, never falling along the last dimension, each value on 1 to 256 neighbouring positions
- query_mask: int32 [256, 32], replicated, may hold values from 0 to 1, as said below
- positives: int32 [256], replicated, may hold values from 0 to 15
- top_index: int32 [256, 16, 8], P(None, 'wide'), may hold values from 0 to 511
- query_weight: bfloat16 [768, 768], replicated, may hold values from -0.02734375 to 0.02734375
- key_weight: bfloat16 [768, 768], replicated, may hold values from -0.21875 to 0.21875
- value_weight: bfloat16 [768, 768], replicated, may hold values from -0.21875 to 0.21875
- output_weight: bfloat16 [768, 768], replicated, may hold values from -1.25 to 1.25
- gate_weight: bfloat16 [768, 2048], replicated, may hold values from -0.21875 to 0.21875
- up_weight: bfloat16 [768, 2048], replicated, may hold values from -0.21875 to 0.21875
- down_weight: bfloat16 [2048, 768], replicated, may hold values from -0.125 to 0.125
- projection: bfloat16 [768, 128], replicated, may hold values from -0.21875 to 0.21875
- attention_gain: float32 [768], replicated, may hold values from 0.5 to 1.5
- feedforward_gain: float32 [768], replicated, may hold values from 0.5 to 1.5
- final_gain: float32 [768], replicated, may hold values from 0.5 to 1.5
- bias_table: float32 [32, 12], replicated, may hold values from -4 to 4
Outputs:
- query_loss: float32 [256], P('wide')
- grad_tokens: float32 [2, 16, 512, 768], P('stream', 'wide')
- grad_query_weight: float32 [768, 768], P('wide')
- grad_key_weight: float32 [768, 768], P('wide')
- grad_value_weight: float32 [768, 768], P('wide')
- grad_output_weight: float32 [768, 768], P('wide')
- grad_gate_weight: float32 [768, 2048], P('wide')
- grad_up_weight: float32 [768, 2048], P('wide')
- grad_down_weight: float32 [2048, 768], P('wide')
- grad_projection: float32 [768, 128], P('wide')
- grad_attention_gain: float32 [768], P('wide')
- grad_feedforward_gain: float32 [768], P('wide')
- grad_final_gain: float32 [768], P('wide')
- grad_bias_table: float32 [32, 12], replicated
The draws below stay inside these ranges and needn't reach their ends.
Inputs may be any that keep to these rules, and one draw needn't show every extreme that they name: `query_mask`: within each query the ones form a prefix of its 32 tokens; the prefix may be empty. `doc_segments`: along each row the ids start at 0, never fall and step by one; no document is longer than half of 512.
All inputs are finite; a program needn't handle non-finite values.
Results may differ from the reference program's by a relative error of at most 0.028.
Values may be sent and summed in bfloat16 or wider, within the bound.
No kernel may reach another device: no remote copies, remote signals or barrier semaphores. Data moves between devices by JAX's collectives and lax.ppermute only.
A program may use at most 256 MiB of HBM per device.

```python
import math
import jax
import jax.numpy as jnp
import numpy as np
from jax import lax

D = 768
HEADS = 12
HEAD_DIM = 64
FF = 2048
PROJ = 128
BUCKETS = 32
SEQ = 512
QLEN = 32
TOPK = 8
ROWS_ALL = 16
QUERIES = 256


def draw_query_mask(key, part):
    key = jax.random.fold_in(key, 11)
    lengths = jax.random.randint(key, (QUERIES, 1), 0, QLEN + 1)
    return (jnp.arange(QLEN, dtype=jnp.int32)[None, :] < lengths).astype(jnp.int32)


def touch_ends(values, rng, smallest, largest):
    extent = values.shape
    index_at = [jax.random.randint(jax.random.fold_in(rng, axis), (), 0, extent[axis]) for axis in range(len(extent))]
    values = values.at[tuple(index_at)].set(smallest)
    longest = extent.index(max(extent))
    index_at[longest] = (index_at[longest] + 1) % extent[longest]
    return values.at[tuple(index_at)].set(largest)


def shard_levels(own_key, shape, shards, least, high):
    loudness = 1.0
    for axis_at, parts in shards:
        draws = jax.random.uniform(jax.random.fold_in(jax.random.fold_in(own_key, 6), axis_at), (parts,), jnp.float32, least / len(shards), high / len(shards))
        loudness = loudness * jnp.repeat(jnp.exp(draws), shape[axis_at] // parts).reshape((-1,) + (1,) * (len(shape) - 1 - axis_at))
    return loudness


def length_profile(amount, total, bound, skew):
    portions = [(1 << 20) // math.isqrt(grade ** skew) + 1 for grade in range(2, amount + 1)]
    spare, given = total - bound - (amount - 1), [1] * (amount - 1)
    while spare > 0:
        movable = [i for i in range(amount - 1) if given[i] < bound]
        whole, remaining = sum([portions[i] for i in movable]), spare
        for i in movable:
            extra = min(bound - given[i], max(1, remaining * portions[i] // whole), spare)
            given[i] = given[i] + extra
            spare = spare - extra
    return np.array([bound] + given)


def ragged(rng, number_of, total, reach, skew):
    if number_of == 2:
        one = jax.random.randint(rng, (), max(1, total - reach), min(reach, total - 1) + 1)
        return jnp.stack([one, total - one])
    tallies = jnp.asarray(length_profile(number_of, total, reach, skew), jnp.int32)
    twos = (number_of - 1) // 2
    source_of, sink = tallies[1:1 + 2 * twos:2], tallies[2:2 + 2 * twos:2]
    margin = jnp.minimum(source_of - 1, reach - sink)
    moved = jax.random.randint(jax.random.fold_in(rng, 1), (twos,), 0, 1 << 20) % (margin + 1)
    tallies = tallies.at[1:1 + 2 * twos:2].set(source_of - moved).at[2:2 + 2 * twos:2].set(sink + moved)
    return tallies[jax.random.permutation(jax.random.fold_in(rng, 2), number_of)]


def gaussian(key, shape, width, most, pieces=(), kind=jnp.bfloat16):
    values = jax.random.normal(key, shape, jnp.float32) * width
    if len(pieces) > 0:
        values = shard_levels(key, shape, pieces, -0.22, 0.18) * values
    return jnp.clip(values, min=-most, max=most).astype(kind)


def setup_inputs(seed: int = 0) -> dict:
    arg_keys = jax.random.split(jax.random.key(seed), 18)
    return {
        "tokens": gaussian(arg_keys[0], (2, ROWS_ALL, SEQ, D), 1.0, 6.0, ((0, 2), (1, 16))),
        "doc_segments": jax.vmap(lambda own: jnp.searchsorted(jnp.cumsum(ragged(own, 4, SEQ, SEQ // 2, 0)), jnp.arange(SEQ), side="right"))(jax.random.split(arg_keys[1], ROWS_ALL)).reshape((ROWS_ALL, SEQ)).astype(jnp.int32),
        "query_mask": draw_query_mask(jax.random.fold_in(arg_keys[17], 71), 0),
        "positives": touch_ends(jax.random.randint(arg_keys[3], (QUERIES,), 0, ROWS_ALL), jax.random.fold_in(arg_keys[3], 1), 0, ROWS_ALL - 1).astype(jnp.int32),
        "top_index": touch_ends(jax.random.randint(arg_keys[4], (QUERIES, ROWS_ALL, TOPK), 0, SEQ), jax.random.fold_in(arg_keys[4], 1), 0, SEQ - 1).astype(jnp.int32),
        "query_weight": gaussian(arg_keys[5], (D, D), (D * HEAD_DIM) ** -0.5, 0.02734375),
        "key_weight": gaussian(arg_keys[6], (D, D), D ** -0.5, 0.21875),
        "value_weight": gaussian(arg_keys[7], (D, D), D ** -0.5, 0.21875),
        "output_weight": gaussian(arg_keys[8], (D, D), (D // 32) ** -0.5, 1.25),
        "gate_weight": gaussian(arg_keys[9], (D, FF), D ** -0.5, 0.21875),
        "up_weight": gaussian(arg_keys[10], (D, FF), D ** -0.5, 0.21875),
        "down_weight": gaussian(arg_keys[11], (FF, D), FF ** -0.5, 0.125),
        "projection": gaussian(arg_keys[12], (D, PROJ), D ** -0.5, 0.21875),
        "attention_gain": jnp.clip(1.0 + 0.1 * jax.random.normal(arg_keys[13], (D,), jnp.float32), 0.5, 1.5),
        "feedforward_gain": jnp.clip(1.0 + 0.1 * jax.random.normal(arg_keys[14], (D,), jnp.float32), 0.5, 1.5),
        "final_gain": jnp.clip(1.0 + 0.1 * jax.random.normal(arg_keys[15], (D,), jnp.float32), 0.5, 1.5),
        "bias_table": gaussian(arg_keys[16], (BUCKETS, HEADS), 1.0, 4.0, (), jnp.float32),
    }


@jax.custom_vjp
def low(v):
    return lax.optimization_barrier(v.astype(jnp.bfloat16)).astype(jnp.float32)

@jax.custom_vjp
def low_back(v):
    return v

def low_keep(v):
    return (low(v), None)

def low_pass(kept, grad):
    return (grad,)

def back_keep(v):
    return (v, None)

def back_low(kept, grad):
    return (low(grad),)
low.defvjp(low_keep, low_pass)
low_back.defvjp(back_keep, back_low)
EPSILON = 1e-06
SOFTMAX_TEMP = 0.05
MASKED_SCORE = -1e+30
HIGHEST = lax.Precision.HIGHEST

def bucket_of(offset):
    distance = jnp.abs(offset)
    far_bucket = jnp.full(offset.shape, 8, jnp.int32)
    for exponent in range(1, 8):
        far_bucket = far_bucket + (distance * distance >= 64 * 2 ** exponent).astype(jnp.int32)
    near_bucket = jnp.where(distance < 8, distance, far_bucket)
    return near_bucket + 16 * (offset > 0).astype(jnp.int32)

def rms_norm(values, gain_vector):
    inverse_rms = lax.rsqrt(lax.optimization_barrier(jnp.mean(values * values, axis=-1, keepdims=True)) + EPSILON)
    return values * inverse_rms * gain_vector

def encode_block(params, block_data):
    row_block, segment = block_data
    query_weight, key_weight, value_weight, output_weight, gate_weight, up_weight, down_weight, projection, attention_gain, feedforward_gain, final_gain, bias_table = params
    block_rows = row_block.shape[0]
    normed = low(rms_norm(row_block, attention_gain))

    def project(matrix):
        return low(low_back(jnp.einsum('bsd,de->bse', normed, matrix, precision=HIGHEST)))
    heads_of_query = project(query_weight).reshape(block_rows, SEQ, HEADS, HEAD_DIM)
    key_heads = project(key_weight).reshape(block_rows, SEQ, HEADS, HEAD_DIM)
    value_heads = project(value_weight).reshape(block_rows, SEQ, HEADS, HEAD_DIM)
    offsets = jnp.arange(SEQ, dtype=jnp.int32)[None, :] - jnp.arange(SEQ, dtype=jnp.int32)[:, None]
    pair_bias = jnp.transpose(bias_table[bucket_of(offsets)], (2, 0, 1))
    raw_scores = jnp.einsum('bihd,bjhd->bhij', heads_of_query, key_heads, precision=HIGHEST) + pair_bias[None]
    scores = low_back(raw_scores)
    same_doc = segment[:, :, None] == segment[:, None, :]
    softmaxed = jax.nn.softmax(jnp.where(same_doc[:, None], scores, MASKED_SCORE), axis=-1)
    context = low(low_back(jnp.einsum('bhij,bjhd->bihd', low(softmaxed), value_heads, precision=HIGHEST)))
    attended = low_back(jnp.einsum('bse,ed->bsd', context.reshape(block_rows, SEQ, D), output_weight, precision=HIGHEST))
    middle = row_block + attended
    normed_two = low(rms_norm(middle, feedforward_gain))
    gate_values = low_back(jnp.einsum('bsd,df->bsf', normed_two, gate_weight, precision=HIGHEST))
    up_values = low_back(jnp.einsum('bsd,df->bsf', normed_two, up_weight, precision=HIGHEST))
    hidden = low(jax.nn.gelu(gate_values, approximate=True) * up_values)
    block_out = middle + low_back(jnp.einsum('bsf,fd->bsd', hidden, down_weight, precision=HIGHEST))
    normed_three = low(rms_norm(block_out, final_gain))
    return low(low_back(jnp.einsum('bsd,dp->bsp', normed_three, projection, precision=HIGHEST)))

def encode(params, all_rows, all_segments):
    blocks = all_rows.shape[0] // 8
    reshaped_rows = all_rows.reshape(blocks, 8, SEQ, D)
    shaped_segments = all_segments.reshape(blocks, 8, SEQ)

    def one_block(block_data):
        return encode_block(params, block_data)
    embedded = lax.map(jax.checkpoint(one_block), (reshaped_rows, shaped_segments))
    return embedded.reshape(all_rows.shape[0], SEQ, PROJ)

def score_all(query_emb, doc_emb, query_mask, top_index):
    token_weight = query_mask.astype(jnp.float32)
    counts = jnp.maximum(lax.optimization_barrier(jnp.sum(token_weight, axis=-1)), 1.0)
    inverse = 1.0 / math.sqrt(PROJ)

    def one_doc(doc_data):
        doc_row, chosen = doc_data
        picked = doc_row[chosen]
        token_scores = low_back(jnp.einsum('qip,qkp->qik', query_emb, picked, precision=HIGHEST) * inverse)
        best_match = jax.nn.logsumexp(token_scores, axis=-1)
        return lax.optimization_barrier(jnp.sum(best_match * token_weight, axis=-1)) / counts
    columns = lax.map(jax.checkpoint(one_doc), (doc_emb, jnp.swapaxes(top_index, 0, 1)))
    return columns.T

def reference(tokens, doc_segments, query_mask, positives, top_index, query_weight, key_weight, value_weight, output_weight, gate_weight, up_weight, down_weight, projection, attention_gain, feedforward_gain, final_gain, bias_table):
    params = tuple((argument.astype(jnp.float32) for argument in (query_weight, key_weight, value_weight, output_weight, gate_weight, up_weight, down_weight, projection, attention_gain, feedforward_gain, final_gain, bias_table)))
    query_segs = jnp.broadcast_to((jnp.arange(SEQ, dtype=jnp.int32) // QLEN)[None, :], (ROWS_ALL, SEQ))
    all_segments = jnp.concatenate([query_segs, doc_segments.astype(jnp.int32)], axis=0)

    def forward(token_values, weights):
        embedded = encode(weights, token_values.reshape(2 * ROWS_ALL, SEQ, D), all_segments)
        query_emb = embedded[:ROWS_ALL].reshape(QUERIES, QLEN, PROJ)
        document_scores = score_all(query_emb, embedded[ROWS_ALL:], query_mask, top_index)
        score_logits = document_scores / SOFTMAX_TEMP
        chosen = jnp.take_along_axis(score_logits, positives[:, None], axis=1)[:, 0]
        return jax.nn.logsumexp(score_logits, axis=1) - chosen
    query_loss, pullback = jax.vjp(forward, tokens.astype(jnp.float32), params)
    grad_tokens, weight_grads = pullback(jnp.ones_like(query_loss))
    return (query_loss, grad_tokens, weight_grads[0], weight_grads[1], weight_grads[2], weight_grads[3], weight_grads[4], weight_grads[5], weight_grads[6], weight_grads[7], weight_grads[8], weight_grads[9], weight_grads[10], weight_grads[11])
```

```python
from functools import partial
import math

import jax
import jax.numpy as jnp
import numpy as np
from jax import lax
from jax.experimental import pallas as pl
from jax.experimental.pallas import tpu as pltpu
from jax.sharding import PartitionSpec as P

EPSILON = 1e-06
SOFTMAX_TEMP = 0.05
MASKED_SCORE = -1e30
HIGHEST = lax.Precision.HIGHEST
BF16 = jnp.bfloat16
F32 = jnp.float32
NT = (((1,), (1,)), ((), ()))
TN = (((0,), (0,)), ((), ()))
VMEM_BYTES = 60 * 1024 * 1024


def matmul(left, right, dims=(((1,), (0,)), ((), ()))):
    return lax.dot_general(left, right, dims, preferred_element_type=F32)


def flip_stream(block):
    return lax.ppermute(block, "stream", [(0, 1), (1, 0)])


def flip_wide(block, bit):
    devices = range(lax.axis_size("wide"))
    return lax.ppermute(block, "wide", [(i, i ^ (1 << bit)) for i in devices])


def added(kept, received):
    return (kept.astype(F32) + received.astype(F32)).astype(BF16)


def halve_rows(block, bit):
    own = (lax.axis_index("wide") >> bit) & 1
    half = block.shape[0] // 2
    sent = lax.dynamic_slice_in_dim(block, (1 - own) * half, half, 0)
    kept = lax.dynamic_slice_in_dim(block, own * half, half, 0)
    return added(kept, flip_wide(sent, bit))


def halve_columns(block):
    own = lax.axis_index("stream")
    half = block.shape[1] // 2
    sent = lax.dynamic_slice_in_dim(block, (1 - own) * half, half, 1)
    kept = lax.dynamic_slice_in_dim(block, own * half, half, 1)
    return added(kept, flip_stream(sent))


def join_columns(block):
    other = flip_stream(block)
    first = lax.axis_index("stream") == 0
    return jnp.where(first, block, other), jnp.where(first, other, block)


def bits_first(grads, width):
    bits = width.bit_length() - 1
    rows, columns = grads.shape
    shaped = grads.reshape((2,) * bits + (rows // width, columns))
    order = tuple(reversed(range(bits))) + (bits, bits + 1)
    return shaped.transpose(order).reshape(rows, columns)


def reduce_group(grads, width):
    bits = width.bit_length() - 1
    summed = halve_rows(grads, 0)
    columns = summed.shape[1] // 2
    one = halve_rows(halve_columns(summed[:, :columns]), 1)
    two = halve_columns(halve_rows(summed[:, columns:], 1))
    part = jnp.concatenate([one, two], axis=1)
    for bit in range(2, bits):
        part = halve_rows(part, bit)
    left, right = join_columns(part)
    quarter = columns // 2
    return jnp.concatenate(
        [left[:, :quarter], right[:, :quarter], left[:, quarter:], right[:, quarter:]], axis=1
    ).astype(F32)


def bucket_of(offset):
    distance = jnp.abs(offset)
    far_bucket = jnp.full(offset.shape, 8, jnp.int32)
    for exponent in range(1, 8):
        far_bucket = far_bucket + (distance * distance >= 64 * 2**exponent).astype(jnp.int32)
    near_bucket = jnp.where(distance < 8, distance, far_bucket)
    return near_bucket + 16 * (offset > 0).astype(jnp.int32)


def attend_kernel(length, bias_ref, seg_row, seg_col, q_ref, k_ref, v_ref, ctx_ref, probs_ref, mask_ref):
    blocks = length // 128

    @pl.when(pl.program_id(0) == 0)
    def _():
        mask_ref[...] = jnp.where(seg_col[...] == seg_row[...], 0.0, MASKED_SCORE)

    queries, keys, values = q_ref[...], k_ref[...], v_ref[...]
    first = lax.broadcasted_iota(jnp.int32, (1, 128), 1) < 64
    contexts = []
    for head in range(2):
        line = jnp.broadcast_to(bias_ref[0, head : head + 1, :], (128, 2 * length))
        base = pltpu.roll(line, 2 * length - 128, 1, stride=1, stride_axis=0)
        own = jnp.where(first == (head == 0), queries, jnp.zeros_like(queries))
        scores = []
        for a in range(blocks):
            rows = slice(128 * a, 128 * a + 128)
            start = length - 128 - 128 * a
            scores.append(
                matmul(keys[rows], own, NT) + base[:, start : start + length] + mask_ref[rows, :]
            )
        top = scores[0].max(axis=0, keepdims=True)
        for part in scores[1:]:
            top = jnp.maximum(top, part.max(axis=0, keepdims=True))
        total = jnp.zeros_like(top)
        for a in range(blocks):
            scores[a] = jnp.exp(scores[a] - top)
            total = total + scores[a].sum(axis=0, keepdims=True)
        inverse = 1.0 / total
        for a in range(blocks):
            probs_ref[head, 128 * a : 128 * a + 128, :] = (scores[a] * inverse).astype(BF16)
        contexts.append(matmul(probs_ref[head], values, TN))
    ctx_ref[...] = jnp.where(first, contexts[0], contexts[1]).astype(BF16)


def attend(bias_lines, segments, queries, keys, values):
    length, width = queries.shape
    pairs = width // 128
    block = pl.BlockSpec((length, 128), lambda p: (0, p))
    return pl.pallas_call(
        partial(attend_kernel, length),
        grid=(pairs,),
        in_specs=[
            pl.BlockSpec((1, 2, 2 * length), lambda p: (p, 0, 0)),
            pl.BlockSpec((1, length), lambda p: (0, 0)),
            pl.BlockSpec((length, 1), lambda p: (0, 0)),
            block,
            block,
            block,
        ],
        out_specs=[block, pl.BlockSpec((2, length, length), lambda p: (p, 0, 0))],
        out_shape=[
            jax.ShapeDtypeStruct((length, width), BF16),
            jax.ShapeDtypeStruct((2 * pairs, length, length), BF16),
        ],
        scratch_shapes=[pltpu.VMEM((length, length), F32)],
        compiler_params=pltpu.CompilerParams(vmem_limit_bytes=VMEM_BYTES),
        name="attend",
    )(
        bias_lines.reshape(pairs, 2, 2 * length),
        segments.reshape(1, length),
        segments.reshape(length, 1),
        queries,
        keys,
        values,
    )


def attend_back_kernel(length, q_ref, k_ref, v_ref, g_ref, probs_ref, gq_ref, gk_ref, gv_ref, bias_ref, gs_ref, acc_ref):
    blocks = length // 128
    queries, keys, values, grads = q_ref[...], k_ref[...], v_ref[...], g_ref[...]
    first = lax.broadcasted_iota(jnp.int32, (1, 128), 1) < 64
    grad_queries, grad_keys, grad_values = [], [], []
    acc_ref[...] = jnp.zeros_like(acc_ref)
    for head in range(2):
        own = jnp.where(first == (head == 0), grads, jnp.zeros_like(grads))
        inner = jnp.zeros((1, length), F32)
        products = []
        for a in range(blocks):
            rows = slice(128 * a, 128 * a + 128)
            grad_probs = matmul(values[rows], own, NT)
            product = grad_probs * probs_ref[head, rows, :].astype(F32)
            inner = inner + product.sum(axis=0, keepdims=True)
            products.append(product)
        for a in range(blocks):
            rows = slice(128 * a, 128 * a + 128)
            grad_scores = products[a] - probs_ref[head, rows, :].astype(F32) * inner
            gs_ref[rows, :] = grad_scores.astype(BF16)
            start = length - 128 - 128 * a
            acc_ref[head, :, start : start + length] += grad_scores
        grad_values.append(matmul(probs_ref[head], grads))
        grad_keys.append(matmul(gs_ref[...], queries))
        grad_queries.append(matmul(gs_ref[...], keys, TN))
        folded = acc_ref[head, 0:8, :]
        for c in range(1, 16):
            folded = folded + pltpu.roll(acc_ref[head, 8 * c : 8 * c + 8, :], 2 * length - 8 * c, 1)
        bias_ref[0, head] = folded
    gq_ref[...] = jnp.where(first, grad_queries[0], grad_queries[1]).astype(BF16)
    gk_ref[...] = jnp.where(first, grad_keys[0], grad_keys[1]).astype(BF16)
    gv_ref[...] = jnp.where(first, grad_values[0], grad_values[1]).astype(BF16)


def attend_back(queries, keys, values, grads, probs):
    length, width = queries.shape
    pairs = width // 128
    block = pl.BlockSpec((length, 128), lambda p: (0, p))
    out = jax.ShapeDtypeStruct((length, width), BF16)
    return pl.pallas_call(
        partial(attend_back_kernel, length),
        grid=(pairs,),
        in_specs=[block, block, block, block, pl.BlockSpec((2, length, length), lambda p: (p, 0, 0))],
        out_specs=[block, block, block, pl.BlockSpec((1, 2, 8, 2 * length), lambda p: (p, 0, 0, 0))],
        out_shape=[out, out, out, jax.ShapeDtypeStruct((pairs, 2, 8, 2 * length), F32)],
        scratch_shapes=[pltpu.VMEM((length, length), BF16), pltpu.VMEM((2, 128, 2 * length), F32)],
        compiler_params=pltpu.CompilerParams(vmem_limit_bytes=VMEM_BYTES),
        name="attend_back",
    )(queries, keys, values, grads, probs)


def bias_lines_of(bias_table, length):
    offsets = length - jnp.arange(2 * length, dtype=jnp.int32)
    onehot = bucket_of(offsets)[:, None] == jnp.arange(bias_table.shape[0], dtype=jnp.int32)[None, :]
    return jnp.dot(onehot.astype(F32), bias_table, precision=HIGHEST).T


def bias_grad_of(folded, buckets, length):
    heads = folded.shape[0]
    place = jnp.arange(2 * length, dtype=jnp.int32)[None, :] - jnp.arange(8, dtype=jnp.int32)[:, None]
    place = (place + 128) % (2 * length)
    onehot = bucket_of(length - place)[:, :, None] == jnp.arange(buckets, dtype=jnp.int32)
    return jnp.dot(
        folded.reshape(heads, -1), onehot.reshape(-1, buckets).astype(F32), precision=HIGHEST
    ).T


def norm_forward(values, gain_vector):
    inverse_rms = lax.rsqrt(jnp.mean(values * values, axis=-1, keepdims=True) + EPSILON)
    return (values * inverse_rms * gain_vector, inverse_rms)


def norm_backward(values, inverse_rms, gain_vector, upstream):
    weighted = upstream * gain_vector
    row_inner = jnp.mean(weighted * values, axis=-1, keepdims=True)
    scale_cubed = inverse_rms * inverse_rms * inverse_rms
    grad_values = weighted * inverse_rms - values * scale_cubed * row_inner
    return (grad_values, jnp.sum(upstream * values * inverse_rms, axis=0))


def match(query_emb, picked, mask, positive):
    inverse = 1.0 / math.sqrt(query_emb.shape[-1])
    scores = jnp.einsum("aip,bakp->abki", query_emb, picked, preferred_element_type=F32) * inverse
    best = jax.nn.logsumexp(scores, axis=2)
    values = mask.astype(F32)
    weight = values / jnp.maximum(jnp.sum(values, axis=-1, keepdims=True), 1.0)
    logits = jnp.sum(best * weight[:, None, :], axis=-1) / SOFTMAX_TEMP
    partition = jax.nn.logsumexp(logits, axis=1)
    target = (
        jnp.arange(logits.shape[1], dtype=jnp.int32)[None, :] == positive[:, None]
    ).astype(F32)
    losses = partition - jnp.sum(logits * target, axis=1)
    grad_scores = (jnp.exp(logits - partition[:, None]) - target) / SOFTMAX_TEMP
    soft = jnp.exp(scores - best[:, :, None, :])
    grad_tokens = (grad_scores[:, :, None, None] * weight[:, None, None, :] * soft).astype(BF16)
    own = jnp.einsum("abki,bakp->aip", grad_tokens, picked, preferred_element_type=F32) * inverse
    picks = jnp.einsum("abki,aip->bakp", grad_tokens, query_emb, preferred_element_type=F32) * inverse
    return losses, own.astype(BF16), picks.astype(BF16)


def per_device(
    tokens,
    doc_segments,
    query_mask,
    positives,
    top_index,
    query_weight,
    key_weight,
    value_weight,
    output_weight,
    gate_weight,
    up_weight,
    down_weight,
    projection,
    attention_gain,
    feedforward_gain,
    final_gain,
    bias_table,
):
    length, model_width = tokens.shape[2], tokens.shape[3]
    head_count = bias_table.shape[1]
    query_len = query_mask.shape[1]
    embed_width = projection.shape[1]
    top = top_index.shape[2]
    width = lax.axis_size("wide")
    row_queries = length // query_len
    half = row_queries // 2
    stream = lax.axis_index("stream")
    place = lax.axis_index("wide")
    is_query = stream == 0

    inputs = tokens.reshape(length, model_width).astype(F32)
    query_segments = jnp.arange(length, dtype=jnp.int32) // query_len
    segments = jnp.where(is_query, query_segments, doc_segments[0])
    bias_lines = bias_lines_of(bias_table, length)
    normed_one, scale_one = norm_forward(inputs, attention_gain)
    normed_one = normed_one.astype(BF16)
    queries = matmul(normed_one, query_weight).astype(BF16)
    keys = matmul(normed_one, key_weight).astype(BF16)
    values = matmul(normed_one, value_weight).astype(BF16)
    context, probs = attend(bias_lines, segments, queries, keys, values)
    middle = inputs + matmul(context, output_weight)
    normed_two, scale_two = norm_forward(middle, feedforward_gain)
    normed_two = normed_two.astype(BF16)
    gate_values = matmul(normed_two, gate_weight)
    up_values = matmul(normed_two, up_weight)
    gelu_values, gelu_pull = jax.vjp(partial(jax.nn.gelu, approximate=True), gate_values)
    hidden = (gelu_values * up_values).astype(BF16)
    block_out = middle + matmul(hidden, down_weight)
    normed_three, scale_three = norm_forward(block_out, final_gain)
    normed_three = normed_three.astype(BF16)
    embedded = matmul(normed_three, projection).astype(BF16)

    picks = top_index.reshape(width, 2, half, top).transpose(1, 0, 2, 3).reshape(-1)
    onehot = (picks[:, None] == jnp.arange(length, dtype=jnp.int32)[None, :]).astype(BF16)
    picked = matmul(onehot, embedded).astype(BF16)
    other_half = flip_stream(embedded[length // 2 :])
    both = ("stream", "wide")
    gathered = lax.all_to_all(
        picked.reshape(2 * width, half * top, embed_width), both, 0, 0, tiled=True
    )
    query_emb = jnp.where(is_query, embedded[: length // 2], other_half)
    start = place * row_queries + stream * half
    losses, own_grads, pick_grads = match(
        query_emb.reshape(half, query_len, embed_width),
        gathered[width:].reshape(width, half, top, embed_width),
        lax.dynamic_slice_in_dim(query_mask, start, half, 0),
        lax.dynamic_slice_in_dim(positives, start, half, 0),
    )
    pick_grads = pick_grads.reshape(width, half * top, embed_width)
    returned = lax.all_to_all(
        jnp.concatenate([jnp.zeros_like(pick_grads), pick_grads], axis=0), both, 0, 0, tiled=True
    )
    loss_high = losses.astype(BF16)
    loss_low = (losses - loss_high.astype(F32)).astype(BF16)
    other_loss = flip_stream(jnp.stack([loss_high, loss_low])).astype(F32)
    other_loss = other_loss[0] + other_loss[1]
    query_loss = jnp.where(
        is_query,
        jnp.concatenate([losses, other_loss]),
        jnp.concatenate([other_loss, losses]),
    )
    own_grads = own_grads.reshape(length // 2, embed_width)
    other_grads = flip_stream(own_grads)
    doc_grads = matmul(onehot, returned.reshape(-1, embed_width), TN).astype(BF16)
    grad_embedded = jnp.where(
        is_query, jnp.concatenate([own_grads, other_grads], axis=0), doc_grads
    )

    grad_projection = matmul(normed_three, grad_embedded, TN)
    grad_three = matmul(grad_embedded, projection, NT)
    grad_out, grad_final_gain = norm_backward(block_out, scale_three, final_gain, grad_three)
    grad_branch = grad_out.astype(BF16)
    grad_down_weight = matmul(hidden, grad_branch, TN).astype(BF16)
    sum_down = reduce_group(bits_first(grad_down_weight, width), width)
    grad_hidden = matmul(grad_branch, down_weight, NT)
    grad_up_values = (grad_hidden * gelu_values).astype(BF16)
    grad_gate_values = gelu_pull(grad_hidden * up_values)[0].astype(BF16)
    grad_two = matmul(grad_gate_values, gate_weight, NT) + matmul(grad_up_values, up_weight, NT)
    grad_mid, grad_feedforward_gain = norm_backward(middle, scale_two, feedforward_gain, grad_two)
    grad_middle = grad_out + grad_mid
    gains = jnp.stack([grad_final_gain, grad_feedforward_gain], axis=1)
    gains = jnp.pad(gains, ((0, 0), (0, embed_width - 2)))
    feed = jnp.concatenate(
        [
            matmul(normed_two, grad_gate_values, TN).astype(BF16),
            matmul(normed_two, grad_up_values, TN).astype(BF16),
            grad_projection.astype(BF16),
            gains.astype(BF16),
        ],
        axis=1,
    )
    sum_feed = reduce_group(bits_first(feed, width), width)
    grad_attended = grad_middle.astype(BF16)
    grad_context = matmul(grad_attended, output_weight, NT).astype(BF16)
    grad_queries, grad_keys, grad_values, folded = attend_back(
        queries, keys, values, grad_context, probs
    )
    attention = jnp.concatenate(
        [
            matmul(normed_one, grad_queries, TN).astype(BF16),
            matmul(normed_one, grad_keys, TN).astype(BF16),
            matmul(normed_one, grad_values, TN).astype(BF16),
            matmul(context, grad_attended, TN).astype(BF16),
        ],
        axis=1,
    )
    sum_attention = reduce_group(bits_first(attention, width), width)
    grad_table = bias_grad_of(
        folded.reshape(head_count, 8, 2 * length), bias_table.shape[0], length
    )
    grad_one = (
        matmul(grad_queries, query_weight, NT)
        + matmul(grad_keys, key_weight, NT)
        + matmul(grad_values, value_weight, NT)
    )
    grad_input, grad_attention_gain = norm_backward(inputs, scale_one, attention_gain, grad_one)
    grad_tokens = (grad_middle + grad_input).reshape(tokens.shape)
    small = lax.psum(jnp.concatenate([grad_table.reshape(-1), grad_attention_gain]), both)
    table_size = grad_table.size
    own_rows = model_width // width
    sum_gain = lax.dynamic_slice_in_dim(small, table_size + place * own_rows, own_rows, 0)
    hidden_width = gate_weight.shape[1]
    edge = 2 * hidden_width
    return (
        query_loss,
        grad_tokens,
        sum_attention[:, :model_width],
        sum_attention[:, model_width : 2 * model_width],
        sum_attention[:, 2 * model_width : 3 * model_width],
        sum_attention[:, 3 * model_width :],
        sum_feed[:, :hidden_width],
        sum_feed[:, hidden_width:edge],
        sum_down,
        sum_feed[:, edge : edge + embed_width],
        sum_gain,
        sum_feed[:, edge + embed_width + 1],
        sum_feed[:, edge + embed_width],
        small[:table_size].reshape(grad_table.shape),
    )


def solution(mesh):
    rows = P("wide", None)
    in_specs = (
        P("stream", "wide", None, None),
        rows,
        P(),
        P(),
        P(None, "wide", None),
    ) + (P(),) * 12
    out_specs = (P("wide"), P("stream", "wide", None, None)) + (rows,) * 8 + (P("wide"),) * 3 + (P(),)
    return jax.shard_map(
        per_device, mesh=mesh, in_specs=in_specs, out_specs=out_specs, check_vma=False
    )
```

```python
from functools import partial
import math

import jax
import jax.numpy as jnp
import numpy as np
from jax import lax
from jax.experimental import pallas as pl
from jax.experimental.pallas import tpu as pltpu
from jax.sharding import PartitionSpec as P

EPSILON = 1e-06
SOFTMAX_TEMP = 0.05
MASKED_SCORE = -1e30
HIGHEST = lax.Precision.HIGHEST
BF16 = jnp.bfloat16
F32 = jnp.float32
NT = (((1,), (1,)), ((), ()))
TN = (((0,), (0,)), ((), ()))


def matmul(left, right, dims=(((1,), (0,)), ((), ()))):
    return lax.dot_general(left, right, dims, preferred_element_type=F32)


def flip_stream(block):
    return lax.ppermute(block, "stream", [(0, 1), (1, 0)])


def flip_wide(block, bit):
    devices = range(lax.axis_size("wide"))
    return lax.ppermute(block, "wide", [(i, i ^ (1 << bit)) for i in devices])


def added(kept, received):
    return (kept.astype(F32) + received.astype(F32)).astype(BF16)


def blocks_ordered(rows, width, order):
    bits = width.bit_length() - 1
    shaped = rows.reshape((2,) * bits + (rows.shape[0] // width,) + rows.shape[1:])
    axes = tuple(bits - 1 - bit for bit in order) + tuple(range(bits, shaped.ndim))
    return shaped.transpose(axes).reshape(rows.shape)


def halve_rows(block, bit):
    own = (lax.axis_index("wide") >> bit) & 1
    half = block.shape[0] // 2
    sent = lax.dynamic_slice_in_dim(block, (1 - own) * half, half, 0)
    kept = lax.dynamic_slice_in_dim(block, own * half, half, 0)
    return added(kept, flip_wide(sent, bit))


def sum_everywhere(block, width):
    block = block + flip_stream(block)
    for bit in range(width.bit_length() - 1):
        block = block + flip_wide(block, bit)
    return block


class Small:
    def __init__(self, array):
        self.array = array


class Raw:
    def __init__(self, array):
        self.array = array


class Part:
    def __init__(self, array, number, size):
        self.array, self.number, self.size = array, number, size


class Fetched:
    def __init__(self, source, target, semaphores, axis, pieces):
        size = target.shape[axis] // pieces
        at = [(slice(None),) * axis + (pl.ds(i * size, size),) for i in range(pieces)]
        self.target = target
        self.copies = [
            pltpu.make_async_copy(source.at[at[i]], target.at[at[i]], semaphores[i]) for i in range(pieces)
        ]
        for copy in self.copies:
            copy.start()

    def piece(self, i):
        if self.copies[i] is not None:
            self.copies[i].wait()
            self.copies[i] = None
        return self.target

    def ready(self):
        for i in range(len(self.copies)):
            self.piece(i)
        return self.target


class Result:
    def __init__(self, ref, target, semaphores):
        self.ref, self.target, self.semaphores = ref, target, semaphores
        self.copies = []

    def send(self, at=(slice(None),)):
        copy = pltpu.make_async_copy(self.ref.at[at], self.target.at[at], self.semaphores[len(self.copies)])
        copy.start()
        self.copies.append(copy)


def call(kernel, out_shape, scratch=(), name=None, after=(), us=5, pieces=None, raw_results=(), limit=56):
    pieces = pieces or {}

    def built(*operands):
        taken, results = len(operands), len(out_shape)
        arrays, buffers, semaphores = [], [], 0
        for i, operand in enumerate(operands):
            wrapped = isinstance(operand, Small | Raw | Part)
            array = operand.array if wrapped else operand
            arrays.append(array if isinstance(operand, Small) else pltpu.with_memory_space_constraint(array, pltpu.HBM))
            if not isinstance(operand, Small | Raw):
                rows = operand.size if isinstance(operand, Part) else array.shape[0]
                buffers.append(pltpu.VMEM((rows,) + array.shape[1:], array.dtype))
                semaphores += pieces.get(i, (0, 1))[1]
        fetched = len(buffers)
        send_at = semaphores
        for i, out in enumerate(out_shape):
            if i not in raw_results:
                buffers.append(pltpu.VMEM(out.shape, out.dtype))
                semaphores += 4

        def run(*refs):
            outputs = refs[taken + len(after) : taken + len(after) + results]
            rest = refs[taken + len(after) + results :]
            slots, sems, own = rest[: len(buffers)], rest[len(buffers)], rest[len(buffers) + 1 :]
            given, place, at = [], 0, 0
            for i, operand in enumerate(operands):
                if isinstance(operand, Small | Raw):
                    given.append(refs[i])
                    continue
                source = refs[i]
                if isinstance(operand, Part):
                    source = source.at[block_at(operand.number(), operand.size)]
                axis, count = pieces.get(i, (0, 1))
                given.append(Fetched(source, slots[place], [sems.at[at + j] for j in range(count)], axis, count))
                place, at = place + 1, at + count
            made, at = [], send_at
            for i, output in enumerate(outputs):
                if i in raw_results:
                    made.append(output)
                    continue
                made.append(Result(slots[place], output, [sems.at[at + j] for j in range(4)]))
                place, at = place + 1, at + 4
            kernel(*given, *made, *own)
            for operand in given:
                if isinstance(operand, Fetched):
                    operand.ready()
            for i, result in enumerate(made):
                if i not in raw_results:
                    if not result.copies:
                        result.send()
                    for copy in result.copies:
                        copy.wait()

        return pl.pallas_call(
            run,
            in_specs=[pl.BlockSpec(memory_space=pltpu.VMEM if isinstance(x, Small) else pl.ANY) for x in operands]
            + [pl.BlockSpec(memory_space=pl.ANY)] * len(after),
            out_specs=[pl.BlockSpec(memory_space=pl.ANY)] * results,
            out_shape=[pltpu.HBM(x.shape, x.dtype) for x in out_shape],
            scratch_shapes=buffers + [pltpu.SemaphoreType.DMA((max(semaphores, 1),))] + list(scratch),
            compiler_params=pltpu.CompilerParams(vmem_limit_bytes=limit << 20),
            cost_estimate=pl.CostEstimate(flops=0, bytes_accessed=int(us * 3.3e6), transcendentals=0),
            name=name,
        )(*arrays, *after)

    return built


def shape_of(*shape, dtype=BF16):
    return jax.ShapeDtypeStruct(shape, dtype)


def tiles(total, size, body):
    def step(i, carry):
        body(pl.ds(pl.multiple_of(i * size, size), size))
        return carry

    lax.fori_loop(0, total // size, step, 0)


def block_at(index, size):
    return pl.ds(pl.multiple_of(index * size, size), size)


def bit_of_wide(bit):
    return (lax.axis_index("wide") >> bit) & 1


def normed(values, gain):
    inverse = lax.rsqrt(jnp.mean(values * values, axis=-1, keepdims=True) + EPSILON)
    return values * inverse * gain


def norm_back(values, gain, upstream):
    inverse = lax.rsqrt(jnp.mean(values * values, axis=-1, keepdims=True) + EPSILON)
    unit = values * inverse
    weighted = upstream * gain
    inner = jnp.mean(weighted * unit, axis=-1, keepdims=True)
    shares = (upstream * unit).reshape(-1, 8, values.shape[1]).sum(axis=0)
    return (weighted - unit * inner) * inverse, shares


def bucket_of(offset):
    distance = jnp.abs(offset)
    far_bucket = jnp.full(offset.shape, 8, jnp.int32)
    for exponent in range(1, 8):
        far_bucket = far_bucket + (distance * distance >= 64 * 2**exponent).astype(jnp.int32)
    near_bucket = jnp.where(distance < 8, distance, far_bucket)
    return near_bucket + 16 * (offset > 0).astype(jnp.int32)


def line_of(gain_ref):
    return jnp.concatenate([gain_ref[i : i + 1, :] for i in range(gain_ref.shape[0])], axis=1)


def forward_kernel(query_len, part, table_ref, seg_ref, gain1_ref, gain2_ref, gain3_ref, picks_ref, x, wq, wk, wv, wo, wg, wu,
                   wd, proj, n1, q, k, v, ctx, probs_out, mid, n2, up_factor, gate_factor, hidden, out, n3, emb, picked,
                   mask_ref, line_ref, base_ref, score_ref, probs_ref, probs_sem, gate_ref, up_ref):
    x_ref = x.ready()
    length, model = x_ref.shape
    blocks = length // 128
    heads = table_ref.shape[1]
    gain = line_of(gain1_ref)

    def norm(rows):
        n1.ref[rows, :] = normed(x_ref[rows, :].astype(F32), gain).astype(BF16)

    tiles(length, 64, norm)
    n1.send()
    for result, weight in ((q, wq), (k, wk), (v, wv)):
        result.ref[...] = matmul(n1.ref[...], weight.ready()[...]).astype(BF16)
        result.send()

    lane = lax.broadcasted_iota(jnp.int32, (1, length), 1)
    segments = jnp.where(lax.axis_index("stream") == 0, lane // query_len, seg_ref[...])
    for a in range(blocks):
        column = jnp.broadcast_to(segments[:, 128 * a : 128 * a + 128], (128, 128)).T[:, 0:1]
        mask_ref[128 * a : 128 * a + 128, :] = jnp.where(column == segments, 0.0, MASKED_SCORE)
    offsets = length - lax.broadcasted_iota(jnp.int32, (1, 2 * length), 1)
    buckets = lax.broadcasted_iota(jnp.int32, (table_ref.shape[0], 2 * length), 0)
    onehot = jnp.where(bucket_of(offsets) == buckets, 1.0, 0.0)
    lines = lax.dot_general(table_ref[...], onehot, TN, precision=HIGHEST, preferred_element_type=F32)
    for head in range(heads):
        line_ref[head] = lines[head : head + 1, :]
    first = lax.broadcasted_iota(jnp.int32, (1, 128), 1) < 64

    def probs_copy(p):
        at = pl.ds(2 * p, 2)
        return pltpu.make_async_copy(probs_ref.at[at], probs_out.at[at], probs_sem.at[p])

    def pair(p, carry):
        own_lanes = block_at(p, 128)
        queries, keys, values = q.ref[:, own_lanes], k.ref[:, own_lanes], v.ref[:, own_lanes]
        contexts = []
        for head in range(2):
            line = jnp.broadcast_to(line_ref[2 * p + head], (128, 2 * length))
            base_ref[...] = pltpu.roll(line, 2 * length - 128, 1, stride=1, stride_axis=0)
            own = jnp.where(first == (head == 0), queries, jnp.zeros_like(queries))
            score_ref[...] = matmul(keys, own, NT)
            for t in range(blocks):
                lanes = slice(128 * t, 128 * t + 128)
                scores = []
                for a in range(blocks):
                    rows = slice(128 * a, 128 * a + 128)
                    start = length - 128 - 128 * a + 128 * t
                    scores.append(score_ref[rows, lanes] + base_ref[:, start : start + 128] + mask_ref[rows, lanes])
                top = scores[0].max(axis=0, keepdims=True)
                for block in scores[1:]:
                    top = jnp.maximum(top, block.max(axis=0, keepdims=True))
                total = jnp.zeros_like(top)
                for a in range(blocks):
                    scores[a] = jnp.exp(scores[a] - top)
                    total = total + scores[a].sum(axis=0, keepdims=True)
                inverse = 1.0 / total
                for a in range(blocks):
                    probs_ref[2 * p + head, 128 * a : 128 * a + 128, lanes] = (scores[a] * inverse).astype(BF16)
            contexts.append(matmul(probs_ref[2 * p + head], values, TN))
        ctx.ref[:, own_lanes] = jnp.where(first, contexts[0], contexts[1]).astype(BF16)
        probs_copy(p).start()
        return carry

    lax.fori_loop(0, heads // 2, pair, 0)
    ctx.send()
    mid.ref[...] = matmul(ctx.ref[...], wo.ready()[...])
    gain = line_of(gain2_ref)

    def start(rows):
        middle = x_ref[rows, :].astype(F32) + mid.ref[rows, :]
        mid.ref[rows, :] = middle
        n2.ref[rows, :] = normed(middle, gain).astype(BF16)

    tiles(length, 64, start)
    mid.send()
    n2.send()
    scale = math.sqrt(2.0 / math.pi)
    wg_ref, wu_ref = wg.ready(), wu.ready()

    def column(columns):
        gate_ref[...] = matmul(n2.ref[...], wg_ref[:, columns])
        up_ref[...] = matmul(n2.ref[...], wu_ref[:, columns])

        def gelu(rows):
            u, up = gate_ref[rows, :], up_ref[rows, :]
            squared = u * u
            tanh = jnp.tanh(scale * u * (1.0 + 0.044715 * squared))
            gate = 0.5 * (1.0 + tanh)
            slope = gate + 0.5 * u * (1.0 - tanh * tanh) * (scale * (1.0 + 3 * 0.044715 * squared))
            value = u * gate
            up_factor.ref[rows, columns] = value.astype(BF16)
            gate_factor.ref[rows, columns] = (up * slope).astype(BF16)
            hidden.ref[rows, columns] = (value * up).astype(BF16)

        tiles(length, 32, gelu)

    tiles(wg_ref.shape[1], part, column)
    for result in (hidden, up_factor, gate_factor):
        result.send()
    out.ref[...] = matmul(hidden.ref[...], wd.ready()[...])
    gain = line_of(gain3_ref)

    def end(rows):
        value = out.ref[rows, :] + mid.ref[rows, :]
        out.ref[rows, :] = value
        n3.ref[rows, :] = normed(value, gain).astype(BF16)

    tiles(length, 64, end)
    out.send()
    n3.send()
    emb.ref[...] = matmul(n3.ref[...], proj.ready()[...]).astype(BF16)
    emb.send()
    tokens = lax.broadcasted_iota(jnp.int32, (1, 128), 1)

    def pick(i, carry):
        column = jnp.broadcast_to(picks_ref[pl.ds(i, 1), :], (128, 128)).T
        onehot = jnp.concatenate(
            [jnp.where(column == tokens + 128 * t, 1.0, 0.0).astype(BF16) for t in range(blocks)], axis=1
        )
        picked.ref[block_at(i, 128), :] = matmul(onehot, emb.ref[...]).astype(BF16)
        return carry

    lax.fori_loop(0, picks_ref.shape[0], pick, 0)
    picked.send()
    for p in range(heads // 2):
        probs_copy(p).wait()


def turn_kernel(source_ref, *refs):
    count = (len(refs) - 1) // 2
    order_ref = refs[-1]
    size = source_ref.shape[1]
    for i in range(size // 128):
        column = jnp.broadcast_to(source_ref[:, 128 * i : 128 * i + 128], (128, 128)).T
        for j in range(size // 128):
            lane = lax.broadcasted_iota(jnp.int32, (1, 128), 1) + 128 * j
            order_ref[128 * i : 128 * i + 128, 128 * j : 128 * j + 128] = jnp.where(column == lane, 1.0, 0.0).astype(BF16)
    for taken, made in zip(refs[:count], refs[count : 2 * count]):
        made.ref[...] = matmul(order_ref[...], taken.ready()[...], NT).astype(BF16)
        made.send()


def end_back_kernel(picks_ref, own_ref, other_ref, proj_ref, gain_ref, returned, block, n3t, ht,
                    dproj, gout, branch, dgain, sent, emb_ref, onehot_ref):
    length = gout.ref.shape[0]
    half = own_ref.shape[0]
    tokens = lax.broadcasted_iota(jnp.int32, (length, 128), 0)

    def pick(i, carry):
        row = picks_ref[pl.ds(i, 1), :]
        onehot_ref[:, block_at(i, 128)] = jnp.where(row == tokens, 1.0, 0.0).astype(BF16)
        return carry

    lax.fori_loop(0, picks_ref.shape[0], pick, 0)
    is_query = lax.axis_index("stream") == 0
    returned_ref, block_ref, gain = returned.ready(), block.ready(), line_of(gain_ref)
    for side, query_ref in enumerate((own_ref, other_ref)):
        rows = slice(side * half, side * half + half)
        doc = matmul(onehot_ref[rows, :], returned_ref[...]).astype(BF16)
        emb_ref[rows, :] = jnp.where(is_query, query_ref[...], doc)
    gout.ref[...] = matmul(emb_ref[...], proj_ref[...], NT)
    dgain.ref[...] = jnp.zeros_like(dgain.ref)

    def norm(rows):
        grad, shares = norm_back(block_ref[rows, :], gain, gout.ref[rows, :])
        gout.ref[rows, :] = grad
        branch.ref[rows, :] = grad.astype(BF16)
        dgain.ref[...] += shares

    tiles(length, 64, norm)
    gout.send()
    branch.send()
    sent.ref[...] = matmul(ht.ready()[...], branch.ref[...]).astype(BF16)
    sent.send()
    dproj.ref[...] = matmul(n3t.ready()[...], emb_ref[...]).astype(BF16)


def gates_back_kernel(part, branch, wd, upf, gatef, n2t, gg, gu, sg, su, grad_ref):
    branch_ref = branch.ready()
    length = branch_ref.shape[0]
    for i in range(gg.ref.shape[1] // part):
        columns = slice(i * part, i * part + part)
        grad_ref[...] = matmul(branch_ref[...], wd.piece(i)[columns, :], NT)
        upf_ref, gatef_ref = upf.piece(i), gatef.piece(i)

        def factors(rows):
            grad = grad_ref[rows, :]
            gu.ref[rows, columns] = (grad * upf_ref[rows, columns].astype(F32)).astype(BF16)
            gg.ref[rows, columns] = (grad * gatef_ref[rows, columns].astype(F32)).astype(BF16)

        tiles(length, 64, factors)
        n2t_ref = n2t.ready()
        sg.ref[:, columns] = matmul(n2t_ref[...], gg.ref[:, columns]).astype(BF16)
        su.ref[:, columns] = matmul(n2t_ref[...], gu.ref[:, columns]).astype(BF16)
        for result in (sg, su, gg, gu):
            result.send((slice(None), pl.ds(i * part, part)))


def down_keep_kernel(branch, ht, recv, sent, keep):
    half = sent.ref.shape[0]
    own = bit_of_wide(2)
    branch_ref, ht_ref, recv_ref = branch.ready(), ht.ready(), recv.ready()
    for target, side in ((sent, 1 - own), (keep, own)):
        rows = block_at(side, half)
        target.ref[...] = (matmul(ht_ref[rows, :], branch_ref[...]) + recv_ref[rows, :].astype(F32)).astype(BF16)
        target.send()


def gates_keep_kernel(part, n2t, gg, rg, gu, ru, gs, gk, us, uk):
    columns = gs.ref.shape[1]
    quarter = us.ref.shape[0]
    own, stream = bit_of_wide(1), lax.axis_index("stream")
    n2t_ref, gg_ref, rg_ref = n2t.ready(), gg.ready(), rg.ready()
    for target, side in ((gs, 1 - stream), (gk, stream)):
        for i in range(columns // part):
            local = slice(i * part, i * part + part)
            there = block_at(side * (columns // part) + i, part)
            made = matmul(n2t_ref[...], gg_ref[:, there])
            target.ref[:, local] = (made + rg_ref[:, there].astype(F32)).astype(BF16)
        target.send()
    gu_ref, ru_ref = gu.ready(), ru.ready()
    for target, side in ((us, 1 - own), (uk, own)):
        rows = block_at(side, quarter)
        for i in range(gu_ref.shape[1] // part):
            local = slice(i * part, i * part + part)
            made = matmul(n2t_ref[rows, :], gu_ref[:, local])
            target.ref[:, local] = (made + ru_ref[rows, local].astype(F32)).astype(BF16)
        target.send()


def middle_back_kernel(gain_ref, gg, wg, gu, wu, mid, gout, wo, gmid, att, gctx, dgain):
    gmid.ref[...] = matmul(gg.ready()[...], wg.ready()[...], NT)
    gmid.ref[...] += matmul(gu.ready()[...], wu.ready()[...], NT)
    dgain.ref[...] = jnp.zeros_like(dgain.ref)
    mid_ref, gout_ref, gain = mid.ready(), gout.ready(), line_of(gain_ref)

    def norm(rows):
        grad, shares = norm_back(mid_ref[rows, :], gain, gmid.ref[rows, :])
        grad = grad + gout_ref[rows, :]
        gmid.ref[rows, :] = grad
        att.ref[rows, :] = grad.astype(BF16)
        dgain.ref[...] += shares

    tiles(mid_ref.shape[0], 64, norm)
    gmid.send()
    att.send()
    gctx.ref[...] = matmul(att.ref[...], wo.ready()[...], NT).astype(BF16)


def attend_back_kernel(dproj_ref, probs_in, q, k, v, g, n1t, ct, att, gq, gk, gv, bias, sent,
                       probs_ref, probs_sem, gs_ref, gp_ref, acc_ref):
    def probs_copy(p):
        at = pl.ds(2 * p, 2)
        return pltpu.make_async_copy(probs_in.at[at], probs_ref.at[at], probs_sem.at[p])

    pairs = probs_ref.shape[0] // 2
    for p in range(pairs):
        probs_copy(p).start()
    q_ref, k_ref, v_ref, g_ref = q.ready(), k.ready(), v.ready(), g.ready()
    length = q_ref.shape[0]
    blocks = length // 128
    first = lax.broadcasted_iota(jnp.int32, (1, 128), 1) < 64
    acc_ref[:, (2 * blocks - 1) * 128 :] = jnp.zeros((128, 128), F32)

    def pair(p, carry):
        own_lanes = block_at(p, 128)
        queries, keys = q_ref[:, own_lanes], k_ref[:, own_lanes]
        values, grads = v_ref[:, own_lanes], g_ref[:, own_lanes]
        grad_queries, grad_keys, grad_values = [], [], []
        probs_copy(p).wait()
        for head in range(2):
            own = jnp.where(first == (head == 0), grads, jnp.zeros_like(grads))
            gp_ref[...] = matmul(values, own, NT)
            for t in range(blocks):
                lanes = slice(128 * t, 128 * t + 128)
                inner = jnp.zeros((1, 128), F32)
                products = []
                for a in range(blocks):
                    rows = slice(128 * a, 128 * a + 128)
                    product = gp_ref[rows, lanes] * probs_ref[2 * p + head, rows, lanes].astype(F32)
                    inner = inner + product.sum(axis=0, keepdims=True)
                    products.append(product)
                for a in range(blocks):
                    rows = slice(128 * a, 128 * a + 128)
                    grad_scores = products[a] - probs_ref[2 * p + head, rows, lanes].astype(F32) * inner
                    gs_ref[rows, lanes] = grad_scores.astype(BF16)
                    start = length - 128 - 128 * a + 128 * t
                    if t == 0 or a == 0:
                        acc_ref[:, start : start + 128] = grad_scores
                    else:
                        acc_ref[:, start : start + 128] += grad_scores
            grad_values.append(matmul(probs_ref[2 * p + head], grads))
            grad_keys.append(matmul(gs_ref[...], queries))
            grad_queries.append(matmul(gs_ref[...], keys, TN))
            folded = acc_ref[0:8, :]
            for c in range(1, 16):
                folded = folded + pltpu.roll(acc_ref[8 * c : 8 * c + 8, :], 2 * length - 8 * c, 1)
            bias.ref[2 * p + head] = folded
        gq.ref[:, own_lanes] = jnp.where(first, grad_queries[0], grad_queries[1]).astype(BF16)
        gk.ref[:, own_lanes] = jnp.where(first, grad_keys[0], grad_keys[1]).astype(BF16)
        gv.ref[:, own_lanes] = jnp.where(first, grad_values[0], grad_values[1]).astype(BF16)
        return carry

    lax.fori_loop(0, pairs, pair, 0)
    for result in (gq, gk, gv, bias):
        result.send()
    half, model = sent.ref.shape[0], q_ref.shape[1]
    n1t_ref, ct_ref, att_ref = n1t.ready(), ct.ready(), att.ready()
    for place, (left, right) in enumerate(((n1t_ref, gq.ref), (n1t_ref, gk.ref), (n1t_ref, gv.ref), (ct_ref, att_ref))):
        sent.ref[:, place * model : (place + 1) * model] = matmul(left[...], right[...]).astype(BF16)
    sent.ref[:, 4 * model :] = dproj_ref[block_at(1 - bit_of_wide(0), half), :]


def heads_keep_kernel(dproj_ref, share1_ref, share2_ref, share3_ref, n1t, ct, gq, gk, gv, att, recv,
                      asent, akeep, bsent, bkeep, dgain):
    for i, share_ref in enumerate((share1_ref, share2_ref, share3_ref)):
        dgain.ref[i : i + 1, :] = jnp.sum(share_ref[...], axis=0, keepdims=True)
    half, model = asent.ref.shape
    quarter = bsent.ref.shape[0]
    own = bit_of_wide(1)
    n1t_ref, gq_ref, gk_ref, recv_ref = n1t.ready(), gq.ready(), gk.ready(), recv.ready()
    grad_query = (matmul(n1t_ref[...], gq_ref[...]) + recv_ref[:, :model].astype(F32)).astype(BF16)
    grad_key = (matmul(n1t_ref[...], gk_ref[...]) + recv_ref[:, model : 2 * model].astype(F32)).astype(BF16)
    first = lax.axis_index("stream") == 0
    asent.ref[...] = jnp.where(first, grad_key, grad_query)
    asent.send()
    akeep.ref[...] = jnp.where(first, grad_query, grad_key)
    akeep.send()
    ct_ref, gv_ref, att_ref = ct.ready(), gv.ready(), att.ready()
    for target, side in ((bsent, 1 - own), (bkeep, own)):
        rows = block_at(side, quarter)
        arrived = recv_ref[rows, 2 * model : 3 * model].astype(F32)
        target.ref[:, :model] = (matmul(n1t_ref[rows, :], gv_ref[...]) + arrived).astype(BF16)
        arrived = recv_ref[rows, 3 * model : 4 * model].astype(F32)
        target.ref[:, model : 2 * model] = (matmul(ct_ref[rows, :], att_ref[...]) + arrived).astype(BF16)
        arrived = recv_ref[rows, 4 * model :].astype(F32)
        mine = dproj_ref[block_at(2 * bit_of_wide(0) + side, quarter), :].astype(F32)
        target.ref[:, 2 * model :] = (mine + arrived).astype(BF16)
        target.send()


def start_back_kernel(gain_ref, gq, wq, gk, wk, gv, wv, x, gmid, tok, dgain):
    tok.ref[...] = matmul(gq.ready()[...], wq.ready()[...], NT)
    tok.ref[...] += matmul(gk.ready()[...], wk.ready()[...], NT)
    tok.ref[...] += matmul(gv.ready()[...], wv.ready()[...], NT)
    dgain.ref[...] = jnp.zeros_like(dgain.ref)
    x_ref, gmid_ref, gain = x.ready(), gmid.ready(), line_of(gain_ref)
    quarter = x_ref.shape[0] // 4

    def norm(rows):
        grad, shares = norm_back(x_ref[rows, :].astype(F32), gain, tok.ref[rows, :])
        tok.ref[rows, :] = gmid_ref[rows, :] + grad
        dgain.ref[...] += shares

    for i in range(4):
        lax.fori_loop(2 * i, 2 * i + 2, lambda j, c: (norm(block_at(j, quarter // 2)), c)[1], 0)
        tok.send((pl.ds(i * quarter, quarter),))


def bias_grad_of(folded, buckets, length):
    heads = folded.shape[0]
    place = jnp.arange(2 * length, dtype=jnp.int32)[None, :] - jnp.arange(8, dtype=jnp.int32)[:, None]
    place = (place + 128) % (2 * length)
    onehot = bucket_of(length - place)[:, :, None] == jnp.arange(buckets, dtype=jnp.int32)
    return jnp.dot(
        folded.reshape(heads, -1), onehot.reshape(-1, buckets).astype(F32), precision=HIGHEST
    ).T


def match(query_emb, picked, mask, positive):
    inverse = 1.0 / math.sqrt(query_emb.shape[-1])
    scores = jnp.einsum("aip,bakp->abki", query_emb, picked, preferred_element_type=F32) * inverse
    best = jax.nn.logsumexp(scores, axis=2)
    values = mask.astype(F32)
    weight = values / jnp.maximum(jnp.sum(values, axis=-1, keepdims=True), 1.0)
    logits = jnp.sum(best * weight[:, None, :], axis=-1) / SOFTMAX_TEMP
    partition = jax.nn.logsumexp(logits, axis=1)
    target = (
        jnp.arange(logits.shape[1], dtype=jnp.int32)[None, :] == positive[:, None]
    ).astype(F32)
    losses = partition - jnp.sum(logits * target, axis=1)
    grad_scores = (jnp.exp(logits - partition[:, None]) - target) / SOFTMAX_TEMP
    soft = jnp.exp(scores - best[:, :, None, :])
    grad_tokens = (grad_scores[:, :, None, None] * weight[:, None, None, :] * soft).astype(BF16)
    own = jnp.einsum("abki,bakp->aip", grad_tokens, picked, preferred_element_type=F32) * inverse
    picks = jnp.einsum("abki,aip->bakp", grad_tokens, query_emb, preferred_element_type=F32) * inverse
    return losses, own.astype(BF16), picks.astype(BF16)


def per_device(
    tokens,
    doc_segments,
    query_mask,
    positives,
    top_index,
    query_weight,
    key_weight,
    value_weight,
    output_weight,
    gate_weight,
    up_weight,
    down_weight,
    projection,
    attention_gain,
    feedforward_gain,
    final_gain,
    bias_table,
):
    length, model = tokens.shape[2], tokens.shape[3]
    heads = bias_table.shape[1]
    query_len = query_mask.shape[1]
    embed = projection.shape[1]
    hidden_width = gate_weight.shape[1]
    top = top_index.shape[2]
    width = lax.axis_size("wide")
    bits = width.bit_length() - 1
    row_queries = length // query_len
    half = row_queries // 2
    stream = lax.axis_index("stream")
    place = lax.axis_index("wide")
    is_query = stream == 0
    gain1, gain2, gain3 = (Small(g.reshape(-1, 128)) for g in (attention_gain, feedforward_gain, final_gain))
    part = 512
    order = tuple(range(bits))
    down_order = (0, 2, 1) + order[3:]

    inputs = tokens.reshape(length, model)
    flat = shape_of(length, model)
    flat32 = shape_of(length, model, dtype=F32)
    wide_flat = shape_of(length, hidden_width)
    shares = shape_of(8, model, dtype=F32)
    square = pltpu.VMEM((length, length), F32)
    pair_sems = pltpu.SemaphoreType.DMA((heads // 2,))
    all_probs = pltpu.VMEM((heads, length, length), BF16)
    picks = top_index.reshape(width, 2, half, top).transpose(1, 0, 2, 3).reshape(-1, 128)
    (
        normed_one, queries, keys, values, context, probs, middle, normed_two, up_factor, gate_factor, hidden, block_out,
        normed_three, embedded, picked,
    ) = call(
        partial(forward_kernel, query_len, part),
        [flat] * 5 + [shape_of(heads, length, length), flat32, flat, wide_flat, wide_flat, wide_flat, flat32, flat,
         shape_of(length, embed), shape_of(picks.size, embed)],
        scratch=[
            square, pltpu.VMEM((heads, 1, 2 * length), F32), pltpu.VMEM((128, 2 * length), F32), square, all_probs,
            pair_sems, pltpu.VMEM((length, part), F32), pltpu.VMEM((length, part), F32),
        ],
        name="forward", us=25, raw_results=(5,),
    )(
        Small(bias_table), Small(doc_segments), gain1, gain2, gain3, Small(picks), inputs, query_weight, key_weight,
        value_weight, output_weight, gate_weight, up_weight, down_weight, projection,
    )

    other_half = flip_stream(embedded[length // 2 :])
    both = ("stream", "wide")
    gathered = lax.all_to_all(picked.reshape(2 * width, half * top, embed), both, 0, 0, tiled=True)
    query_emb = jnp.where(is_query, embedded[: length // 2], other_half)
    start = place * row_queries + stream * half
    losses, own_grads, pick_grads = match(
        query_emb.reshape(half, query_len, embed),
        gathered[width:].reshape(width, half, top, embed),
        lax.dynamic_slice_in_dim(query_mask, start, half, 0),
        lax.dynamic_slice_in_dim(positives, start, half, 0),
    )
    pick_grads = pick_grads.reshape(width, half * top, embed)
    returned = lax.all_to_all(
        jnp.concatenate([jnp.zeros_like(pick_grads), pick_grads], axis=0), both, 0, 0, tiled=True
    )
    loss_high = losses.astype(BF16)
    loss_low = (losses - loss_high.astype(F32)).astype(BF16)
    other_loss = flip_stream(jnp.stack([loss_high, loss_low])).astype(F32)
    other_loss = other_loss[0] + other_loss[1]
    query_loss = jnp.where(
        is_query,
        jnp.concatenate([losses, other_loss]),
        jnp.concatenate([other_loss, losses]),
    )
    own_grads = own_grads.reshape(length // 2, embed)
    other_grads = flip_stream(own_grads)

    source = blocks_ordered(jnp.arange(model, dtype=jnp.int32), width, order).reshape(1, model)
    tall = shape_of(model, length)
    n1_t, n2_t, n3_t, context_t = call(
        turn_kernel, [tall] * 4, scratch=[pltpu.VMEM((model, model), BF16)], name="turn", us=4
    )(Small(source), normed_one, normed_two, normed_three, context)
    hidden_t = blocks_ordered(hidden.T, width, down_order)

    def core():
        return bit_of_wide(0)

    def other_core():
        return 1 - bit_of_wide(0)

    grad_projection, grad_out, branch, shares3, down_send = call(
        end_back_kernel,
        [shape_of(model, embed), flat32, flat, shares, shape_of(hidden_width // 2, model)],
        scratch=[pltpu.VMEM((length, embed), BF16), pltpu.VMEM((length, picks.size), BF16)],
        name="end_back", us=6, after=(other_loss,),
    )(
        Small(picks), Small(own_grads), Small(other_grads), Small(projection), gain3, returned.reshape(-1, embed), block_out,
        n3_t, Part(hidden_t, other_core, hidden_width // 2),
    )
    down_recv = flip_wide(down_send, 0)

    half_rows = shape_of(model // 2, hidden_width)
    grad_gate, grad_up, gate_send, up_send = call(
        partial(gates_back_kernel, part), [wide_flat, wide_flat, half_rows, half_rows],
        scratch=[pltpu.VMEM((length, part), F32)],
        name="gates_back", us=7, pieces={1: (0, 4), 2: (1, 4), 3: (1, 4)},
    )(branch, down_weight, up_factor, gate_factor, Part(n2_t, other_core, model // 2))
    gate_recv = flip_wide(gate_send, 0)
    up_recv = flip_wide(up_send, 0)

    down_send, down_keep = call(
        down_keep_kernel, [shape_of(hidden_width // 4, model)] * 2, name="down_keep", us=3, after=(gate_send,)
    )(branch, Part(hidden_t, core, hidden_width // 2), down_recv)
    down_recv = flip_wide(down_send, 2)

    grad_middle, attended, grad_context, shares2 = call(
        middle_back_kernel, [flat32, flat, flat, shares], name="middle_back", us=8, after=(down_keep, gate_recv, up_recv),
    )(gain2, grad_gate, gate_weight, grad_up, up_weight, middle, grad_out, output_weight)

    gate_send, gate_keep, up_send, up_keep = call(
        partial(gates_keep_kernel, part),
        [shape_of(model // 2, hidden_width // 2)] * 2 + [shape_of(model // 4, hidden_width)] * 2,
        name="gates_keep", us=5, after=(shares2,),
    )(Part(n2_t, core, model // 2), grad_gate, gate_recv, grad_up, up_recv)
    gate_recv = flip_stream(gate_send)
    up_recv = flip_wide(up_send, 1)

    widest = 4 * model + embed
    grad_queries, grad_keys, grad_values, folded, heads_send = call(
        attend_back_kernel,
        [flat, flat, flat, shape_of(heads, 8, 2 * length, dtype=F32), shape_of(model // 2, widest)],
        scratch=[all_probs, pair_sems, pltpu.VMEM((length, length), BF16), square, pltpu.VMEM((128, 2 * length), F32)],
        name="attend_back", us=14, after=(up_keep, down_recv),
    )(
        Small(grad_projection), Raw(probs), queries, keys, values, grad_context, Part(n1_t, other_core, model // 2),
        Part(context_t, other_core, model // 2), attended,
    )
    down_sum = halve_rows(added(down_keep, down_recv), 1)
    heads_recv = flip_wide(heads_send, 0)
    gate_sum = added(gate_keep, gate_recv)
    up_sum = added(up_keep, up_recv)
    grad_tokens, shares1 = call(
        start_back_kernel, [flat32, shares], name="start_back", us=5, after=(heads_send, down_sum, gate_recv, up_recv)
    )(gain1, grad_queries, query_weight, grad_keys, key_weight, grad_values, value_weight, inputs, grad_middle)
    a_send, a_keep, b_send, b_keep, gain_grads = call(
        heads_keep_kernel,
        [shape_of(model // 2, model)] * 2 + [shape_of(model // 4, 2 * model + embed)] * 2
        + [shape_of(3, model, dtype=F32)],
        name="heads_keep", us=4, after=(grad_tokens,),
    )(
        Small(grad_projection), Small(shares1), Small(shares2), Small(shares3), Part(n1_t, core, model // 2),
        Part(context_t, core, model // 2), grad_queries, grad_keys, grad_values, attended, heads_recv,
    )
    a_sum = added(a_keep, flip_stream(a_send))
    b_sum = added(b_keep, flip_wide(b_send, 1))

    for bit in down_order[3:]:
        down_sum = halve_rows(down_sum, bit)
    down_sum = down_sum.astype(F32) + flip_stream(down_sum).astype(F32)

    def finish(first, second):
        block = jnp.concatenate([halve_rows(first, 1), second], axis=1)
        for bit in range(2, bits):
            block = halve_rows(block, bit)
        other = flip_stream(block)
        edge = first.shape[1]
        mine, theirs = block[:, :edge].astype(F32), other[:, :edge].astype(F32)
        left, right = jnp.where(is_query, mine, theirs), jnp.where(is_query, theirs, mine)
        return left, right, block[:, edge:].astype(F32) + other[:, edge:].astype(F32)

    gate_left, gate_right, sum_up = finish(gate_sum, up_sum)
    sum_query, sum_key, rest = finish(a_sum, b_sum)
    grad_table = bias_grad_of(folded, bias_table.shape[0], length)
    small = jnp.concatenate([gain_grads.reshape(-1), grad_table.reshape(-1)])
    small = sum_everywhere(small.reshape(-1, 128), width).reshape(-1)
    own_rows = model // width
    grad_gains = [lax.dynamic_slice_in_dim(small, i * model + place * own_rows, own_rows, 0) for i in range(3)]
    return (
        query_loss,
        grad_tokens.reshape(tokens.shape),
        sum_query,
        sum_key,
        rest[:, :model],
        rest[:, model : 2 * model],
        jnp.concatenate([gate_left, gate_right], axis=1),
        sum_up,
        down_sum,
        rest[:, 2 * model :],
        grad_gains[0],
        grad_gains[1],
        grad_gains[2],
        small[3 * model :].reshape(bias_table.shape),
    )


def solution(mesh):
    rows = P("wide", None)
    in_specs = (
        P("stream", "wide", None, None),
        rows,
        P(),
        P(),
        P(None, "wide", None),
    ) + (P(),) * 12
    out_specs = (P("wide"), P("stream", "wide", None, None)) + (rows,) * 8 + (P("wide"),) * 3 + (P(),)
    return jax.shard_map(
        per_device, mesh=mesh, in_specs=in_specs, out_specs=out_specs, check_vma=False
    )
```

```python
from functools import partial
import math

import jax
import jax.numpy as jnp
import numpy as np
from jax import lax
from jax.experimental import pallas as pl
from jax.experimental.pallas import tpu as pltpu
from jax.sharding import PartitionSpec as P

EPSILON = 1e-06
SOFTMAX_TEMP = 0.05
MASKED_SCORE = -1e30
HIGHEST = lax.Precision.HIGHEST
BF16 = jnp.bfloat16
F32 = jnp.float32
NT = (((1,), (1,)), ((), ()))
TN = (((0,), (0,)), ((), ()))


def matmul(left, right, dims=(((1,), (0,)), ((), ()))):
    return lax.dot_general(left, right, dims, preferred_element_type=F32)


def flip_stream(block):
    return lax.ppermute(block, "stream", [(0, 1), (1, 0)])


def flip_wide(block, bit):
    devices = range(lax.axis_size("wide"))
    return lax.ppermute(block, "wide", [(i, i ^ (1 << bit)) for i in devices])


def added(kept, received):
    return (kept.astype(F32) + received.astype(F32)).astype(BF16)


def blocks_ordered(rows, width, order):
    bits = width.bit_length() - 1
    shaped = rows.reshape((2,) * bits + (rows.shape[0] // width,) + rows.shape[1:])
    axes = tuple(bits - 1 - bit for bit in order) + tuple(range(bits, shaped.ndim))
    return shaped.transpose(axes).reshape(rows.shape)


def halve_rows(block, bit):
    own = (lax.axis_index("wide") >> bit) & 1
    half = block.shape[0] // 2
    sent = lax.dynamic_slice_in_dim(block, (1 - own) * half, half, 0)
    kept = lax.dynamic_slice_in_dim(block, own * half, half, 0)
    return added(kept, flip_wide(sent, bit))


def sum_everywhere(block, width):
    block = block + flip_stream(block)
    for bit in range(width.bit_length() - 1):
        block = block + flip_wide(block, bit)
    return block


class Small:
    def __init__(self, array):
        self.array = array


class Raw:
    def __init__(self, array):
        self.array = array


class Part:
    def __init__(self, array, number, size):
        self.array, self.number, self.size = array, number, size


class Fetched:
    def __init__(self, source, target, semaphores, axis, pieces):
        size = target.shape[axis] // pieces
        at = [(slice(None),) * axis + (pl.ds(i * size, size),) for i in range(pieces)]
        self.target = target
        self.copies = [
            pltpu.make_async_copy(source.at[at[i]], target.at[at[i]], semaphores[i]) for i in range(pieces)
        ]
        for copy in self.copies:
            copy.start()

    def piece(self, i):
        if self.copies[i] is not None:
            self.copies[i].wait()
            self.copies[i] = None
        return self.target

    def ready(self):
        for i in range(len(self.copies)):
            self.piece(i)
        return self.target


class Result:
    def __init__(self, ref, target, semaphores):
        self.ref, self.target, self.semaphores = ref, target, semaphores
        self.copies = []

    def send(self, at=(slice(None),)):
        copy = pltpu.make_async_copy(self.ref.at[at], self.target.at[at], self.semaphores[len(self.copies)])
        copy.start()
        self.copies.append(copy)


def call(kernel, out_shape, scratch=(), name=None, after=(), us=5, pieces=None, raw_results=(), limit=56):
    pieces = pieces or {}

    def built(*operands):
        taken, results = len(operands), len(out_shape)
        arrays, buffers, semaphores = [], [], 0
        for i, operand in enumerate(operands):
            wrapped = isinstance(operand, Small | Raw | Part)
            array = operand.array if wrapped else operand
            arrays.append(array if isinstance(operand, Small) else pltpu.with_memory_space_constraint(array, pltpu.HBM))
            if not isinstance(operand, Small | Raw):
                rows = operand.size if isinstance(operand, Part) else array.shape[0]
                buffers.append(pltpu.VMEM((rows,) + array.shape[1:], array.dtype))
                semaphores += pieces.get(i, (0, 1))[1]
        fetched = len(buffers)
        send_at = semaphores
        for i, out in enumerate(out_shape):
            if i not in raw_results:
                buffers.append(pltpu.VMEM(out.shape, out.dtype))
                semaphores += 4

        def run(*refs):
            outputs = refs[taken + len(after) : taken + len(after) + results]
            rest = refs[taken + len(after) + results :]
            slots, sems, own = rest[: len(buffers)], rest[len(buffers)], rest[len(buffers) + 1 :]
            given, place, at = [], 0, 0
            for i, operand in enumerate(operands):
                if isinstance(operand, Small | Raw):
                    given.append(refs[i])
                    continue
                source = refs[i]
                if isinstance(operand, Part):
                    source = source.at[block_at(operand.number(), operand.size)]
                axis, count = pieces.get(i, (0, 1))
                given.append(Fetched(source, slots[place], [sems.at[at + j] for j in range(count)], axis, count))
                place, at = place + 1, at + count
            made, at = [], send_at
            for i, output in enumerate(outputs):
                if i in raw_results:
                    made.append(output)
                    continue
                made.append(Result(slots[place], output, [sems.at[at + j] for j in range(4)]))
                place, at = place + 1, at + 4
            kernel(*given, *made, *own)
            for operand in given:
                if isinstance(operand, Fetched):
                    operand.ready()
            for i, result in enumerate(made):
                if i not in raw_results:
                    if not result.copies:
                        result.send()
                    for copy in result.copies:
                        copy.wait()

        return pl.pallas_call(
            run,
            in_specs=[pl.BlockSpec(memory_space=pltpu.VMEM if isinstance(x, Small) else pl.ANY) for x in operands]
            + [pl.BlockSpec(memory_space=pl.ANY)] * len(after),
            out_specs=[pl.BlockSpec(memory_space=pl.ANY)] * results,
            out_shape=[pltpu.HBM(x.shape, x.dtype) for x in out_shape],
            scratch_shapes=buffers + [pltpu.SemaphoreType.DMA((max(semaphores, 1),))] + list(scratch),
            compiler_params=pltpu.CompilerParams(vmem_limit_bytes=limit << 20),
            cost_estimate=pl.CostEstimate(flops=0, bytes_accessed=int(us * 3.3e6), transcendentals=0),
            name=name,
        )(*arrays, *after)

    return built


def shape_of(*shape, dtype=BF16):
    return jax.ShapeDtypeStruct(shape, dtype)


def tiles(total, size, body):
    def step(i, carry):
        body(pl.ds(pl.multiple_of(i * size, size), size))
        return carry

    lax.fori_loop(0, total // size, step, 0)


def block_at(index, size):
    return pl.ds(pl.multiple_of(index * size, size), size)


def bit_of_wide(bit):
    return (lax.axis_index("wide") >> bit) & 1


def normed(values, gain):
    inverse = lax.rsqrt(jnp.mean(values * values, axis=-1, keepdims=True) + EPSILON)
    return values * inverse * gain


def norm_back(values, gain, upstream):
    inverse = lax.rsqrt(jnp.mean(values * values, axis=-1, keepdims=True) + EPSILON)
    unit = values * inverse
    weighted = upstream * gain
    inner = jnp.mean(weighted * unit, axis=-1, keepdims=True)
    shares = (upstream * unit).reshape(-1, 8, values.shape[1]).sum(axis=0)
    return (weighted - unit * inner) * inverse, shares


def bucket_of(offset):
    distance = jnp.abs(offset)
    far_bucket = jnp.full(offset.shape, 8, jnp.int32)
    for exponent in range(1, 8):
        far_bucket = far_bucket + (distance * distance >= 64 * 2**exponent).astype(jnp.int32)
    near_bucket = jnp.where(distance < 8, distance, far_bucket)
    return near_bucket + 16 * (offset > 0).astype(jnp.int32)


def line_of(gain_ref):
    return jnp.concatenate([gain_ref[i : i + 1, :] for i in range(gain_ref.shape[0])], axis=1)


def forward_kernel(query_len, part, table, seg_ref, gain1_ref, gain2_ref, gain3_ref, picks_ref, x, wq, wk, wv, wo, wg, wu,
                   wd, proj, n1, q, k, v, ctx, probs_out, mid, n2, up_factor, gate_factor, hidden, out, n3, lower, upper, picked,
                   mask_ref, line_ref, base_ref, score_ref, probs_ref, probs_sem, gate_ref, up_ref, emb_ref):
    x_ref = x.ready()
    length, model = x_ref.shape
    blocks = length // 128
    table_ref = table.target
    heads = table_ref.shape[0]
    gain = line_of(gain1_ref)

    def norm(rows):
        n1.ref[rows, :] = normed(x_ref[rows, :].astype(F32), gain).astype(BF16)

    tiles(length, 256, norm)
    n1.send()
    for result, weight in ((q, wq), (k, wk), (v, wv)):
        result.ref[...] = matmul(n1.ref[...], weight.ready()[...]).astype(BF16)
        result.send()

    lane = lax.broadcasted_iota(jnp.int32, (1, length), 1)
    segments = jnp.where(lax.axis_index("stream") == 0, lane // query_len, seg_ref[...])
    for a in range(blocks):
        column = jnp.broadcast_to(segments[:, 128 * a : 128 * a + 128], (128, 128)).T[:, 0:1]
        mask_ref[128 * a : 128 * a + 128, :] = jnp.where(column == segments, 0.0, MASKED_SCORE)
    offsets = length - lax.broadcasted_iota(jnp.int32, (1, 2 * length), 1)
    buckets = lax.broadcasted_iota(jnp.int32, (table_ref.shape[1], 2 * length), 0)
    onehot = jnp.where(bucket_of(offsets) == buckets, 1.0, 0.0)
    lines = jnp.dot(table.ready()[...], onehot, precision=HIGHEST, preferred_element_type=F32)
    for head in range(heads):
        line_ref[head] = lines[head : head + 1, :]
    first = lax.broadcasted_iota(jnp.int32, (1, 128), 1) < 64

    def probs_copy(p):
        at = pl.ds(2 * p, 2)
        return pltpu.make_async_copy(probs_ref.at[at], probs_out.at[at], probs_sem.at[p])

    def pair(p, carry):
        own_lanes = block_at(p, 128)
        queries, keys, values = q.ref[:, own_lanes], k.ref[:, own_lanes], v.ref[:, own_lanes]
        contexts = []
        for head in range(2):
            line = jnp.broadcast_to(line_ref[2 * p + head], (128, 2 * length))
            base_ref[head] = pltpu.roll(line, 2 * length - 128, 1, stride=1, stride_axis=0)
            own = jnp.where(first == (head == 0), queries, jnp.zeros_like(queries))
            score_ref[head] = matmul(keys, own, NT)
            for t in range(blocks):
                lanes = slice(128 * t, 128 * t + 128)
                scores = []
                for a in range(blocks):
                    rows = slice(128 * a, 128 * a + 128)
                    start = length - 128 - 128 * a + 128 * t
                    scores.append(score_ref[head, rows, lanes] + base_ref[head, :, start : start + 128] + mask_ref[rows, lanes])
                top = scores[0].max(axis=0, keepdims=True)
                for block in scores[1:]:
                    top = jnp.maximum(top, block.max(axis=0, keepdims=True))
                total = jnp.zeros_like(top)
                for a in range(blocks):
                    scores[a] = jnp.exp(scores[a] - top)
                    total = total + scores[a].sum(axis=0, keepdims=True)
                inverse = 1.0 / total
                for a in range(blocks):
                    probs_ref[2 * p + head, 128 * a : 128 * a + 128, lanes] = (scores[a] * inverse).astype(BF16)
            contexts.append(matmul(probs_ref[2 * p + head], values, TN))
        ctx.ref[:, own_lanes] = jnp.where(first, contexts[0], contexts[1]).astype(BF16)
        probs_copy(p).start()
        return carry

    lax.fori_loop(0, heads // 2, pair, 0)
    ctx.send()
    mid.ref[...] = matmul(ctx.ref[...], wo.ready()[...])
    gain = line_of(gain2_ref)

    def start(rows):
        middle = x_ref[rows, :].astype(F32) + mid.ref[rows, :]
        mid.ref[rows, :] = middle
        n2.ref[rows, :] = normed(middle, gain).astype(BF16)

    tiles(length, 256, start)
    mid.send()
    n2.send()
    scale = math.sqrt(2.0 / math.pi)
    wg_ref, wu_ref = wg.ready(), wu.ready()

    def column(columns):
        gate_ref[...] = matmul(n2.ref[...], wg_ref[:, columns])
        up_ref[...] = matmul(n2.ref[...], wu_ref[:, columns])

        def gelu(rows):
            u, up = gate_ref[rows, :], up_ref[rows, :]
            squared = u * u
            tanh = jnp.tanh(scale * u * (1.0 + 0.044715 * squared))
            gate = 0.5 * (1.0 + tanh)
            slope = gate + 0.5 * u * (1.0 - tanh * tanh) * (scale * (1.0 + 3 * 0.044715 * squared))
            value = u * gate
            up_factor.ref[rows, columns] = value.astype(BF16)
            gate_factor.ref[rows, columns] = (up * slope).astype(BF16)
            hidden.ref[rows, columns] = (value * up).astype(BF16)

        tiles(length, 32, gelu)

    tiles(wg_ref.shape[1], part, column)
    for result in (hidden, up_factor, gate_factor):
        result.send()
    out.ref[...] = matmul(hidden.ref[...], wd.ready()[...])
    gain = line_of(gain3_ref)

    def end(rows):
        value = out.ref[rows, :] + mid.ref[rows, :]
        out.ref[rows, :] = value
        n3.ref[rows, :] = normed(value, gain).astype(BF16)

    tiles(length, 256, end)
    out.send()
    n3.send()
    emb_ref[...] = matmul(n3.ref[...], proj.ready()[...]).astype(BF16)
    lower.ref[...] = emb_ref[: length // 2, :]
    upper.ref[...] = emb_ref[length // 2 :, :]
    lower.send()
    upper.send()
    tokens = lax.broadcasted_iota(jnp.int32, (1, 128), 1)

    def pick(i, carry):
        column = jnp.broadcast_to(picks_ref[pl.ds(i, 1), :], (128, 128)).T
        onehot = jnp.concatenate(
            [jnp.where(column == tokens + 128 * t, 1.0, 0.0).astype(BF16) for t in range(blocks)], axis=1
        )
        picked.ref[block_at(i, 128), :] = matmul(onehot, emb_ref[...]).astype(BF16)
        return carry

    lax.fori_loop(0, picks_ref.shape[0], pick, 0, unroll=8 if picks_ref.shape[0] % 8 == 0 else 1)
    picked.send()
    for p in range(heads // 2):
        probs_copy(p).wait()


def turn_kernel(source_ref, picks_ref, *refs):
    onehot, refs = refs[-2], refs[:-2] + refs[-1:]
    count = (len(refs) - 1) // 2
    tokens = lax.broadcasted_iota(jnp.int32, (onehot.ref.shape[0], 128), 0)

    def pick(i, carry):
        onehot.ref[:, block_at(i, 128)] = jnp.where(picks_ref[pl.ds(i, 1), :] == tokens, 1.0, 0.0).astype(BF16)
        return carry

    lax.fori_loop(0, picks_ref.shape[0], pick, 0)
    onehot.send()
    order_ref = refs[-1]
    size = source_ref.shape[1]
    for i in range(size // 128):
        column = jnp.broadcast_to(source_ref[:, 128 * i : 128 * i + 128], (128, 128)).T
        for j in range(size // 128):
            lane = lax.broadcasted_iota(jnp.int32, (1, 128), 1) + 128 * j
            order_ref[128 * i : 128 * i + 128, 128 * j : 128 * j + 128] = jnp.where(column == lane, 1.0, 0.0).astype(BF16)
    for taken, made in zip(refs[:count], refs[count : 2 * count]):
        made.ref[...] = matmul(order_ref[...], taken.ready()[...], NT).astype(BF16)
        made.send()


def upper_back_kernel(part, proj_ref, gain2_ref, gain3_ref, own, other, returned, onehot, block, ht, wd, upf, gatef,
                      n2t, n3t, wg, wu, mid, wo, dsent, branch, gg, gu, sg, su, dproj, gmid, att, gctx, dgain2, dgain3,
                      emb_ref, gout_ref, grad_ref, doc_ref, piece_ref=None, piece_sem=None):
    length = gmid.ref.shape[0]
    half = length // 2
    is_query = lax.axis_index("stream") == 0
    returned_ref = returned.ready()
    if isinstance(onehot, Fetched):
        doc_ref[...] = matmul(onehot.ready()[...], returned_ref[...])
    else:
        size = piece_ref.shape[1]
        doc_ref[...] = jnp.zeros_like(doc_ref)

        def add(i, carry):
            copy = pltpu.make_async_copy(onehot.at[:, block_at(i, size)], piece_ref, piece_sem)
            copy.start()
            copy.wait()
            doc_ref[...] += matmul(piece_ref[...], returned_ref[block_at(i, size), :])
            return carry

        lax.fori_loop(0, returned_ref.shape[0] // size, add, 0)
    for side, query in enumerate((own, other)):
        rows = slice(side * half, side * half + half)
        emb_ref[rows, :] = jnp.where(is_query, query.ready()[...], doc_ref[rows, :].astype(BF16))
    gout_ref[...] = matmul(emb_ref[...], proj_ref[...], NT)
    dgain2.ref[...] = jnp.zeros_like(dgain2.ref)
    dgain3.ref[...] = jnp.zeros_like(dgain3.ref)
    block_ref, gain3 = block.ready(), line_of(gain3_ref)

    def norm3(rows):
        grad, shares = norm_back(block_ref[rows, :], gain3, gout_ref[rows, :])
        dgain3.ref[...] += shares
        gout_ref[rows, :] = grad
        branch.ref[rows, :] = grad.astype(BF16)

    tiles(length, 256, norm3)
    branch.send()
    dsent.ref[...] = matmul(ht.ready()[...], branch.ref[...]).astype(BF16)
    dsent.send()

    for i in range(gg.ref.shape[1] // part):
        columns = slice(i * part, i * part + part)
        grad_ref[...] = matmul(branch.ref[...], wd.piece(i)[columns, :], NT)
        upf_ref, gatef_ref = upf.piece(i), gatef.piece(i)

        def factors(rows):
            grad = grad_ref[rows, :]
            gu.ref[rows, columns] = (grad * upf_ref[rows, columns].astype(F32)).astype(BF16)
            gg.ref[rows, columns] = (grad * gatef_ref[rows, columns].astype(F32)).astype(BF16)

        tiles(length, 64, factors)
        n2t_ref = n2t.ready()
        sg.ref[:, columns] = matmul(n2t_ref[...], gg.ref[:, columns]).astype(BF16)
        su.ref[:, columns] = matmul(n2t_ref[...], gu.ref[:, columns]).astype(BF16)
    gg.send()
    gu.send()
    sg.send()
    dproj.ref[...] = matmul(n3t.ready()[...], emb_ref[...]).astype(BF16)
    dproj.send()
    su.send()

    gmid.ref[...] = matmul(gg.ref[...], wg.ready()[...], NT)
    gmid.ref[...] += matmul(gu.ref[...], wu.ready()[...], NT)
    mid_ref, gain2 = mid.ready(), line_of(gain2_ref)

    def norm2(rows):
        grad, shares = norm_back(mid_ref[rows, :], gain2, gmid.ref[rows, :])
        grad = grad + gout_ref[rows, :]
        dgain2.ref[...] += shares
        gmid.ref[rows, :] = grad
        att.ref[rows, :] = grad.astype(BF16)

    tiles(length, 256, norm2)
    gmid.send()
    att.send()
    gctx.ref[...] = matmul(att.ref[...], wo.ready()[...], NT).astype(BF16)


def down_keep_kernel(branch, ht, recv, sent, keep):
    half = sent.ref.shape[0]
    own = bit_of_wide(2)
    branch_ref, ht_ref, recv_ref = branch.ready(), ht.ready(), recv.ready()
    for target, side in ((sent, 1 - own), (keep, own)):
        rows = block_at(side, half)
        target.ref[...] = (matmul(ht_ref[rows, :], branch_ref[...]) + recv_ref[rows, :].astype(F32)).astype(BF16)
        target.send()


def gates_keep_kernel(part, n2t, gg, rg, gu, ru, gs, gk, us, uk):
    columns = gs.ref.shape[1]
    quarter = us.ref.shape[0]
    own, stream = bit_of_wide(1), lax.axis_index("stream")
    n2t_ref, gg_ref, rg_ref = n2t.ready(), gg.ready(), rg.ready()
    for target, side in ((gs, 1 - stream), (gk, stream)):
        for i in range(columns // part):
            local = slice(i * part, i * part + part)
            there = block_at(side * (columns // part) + i, part)
            made = matmul(n2t_ref[...], gg_ref[:, there])
            target.ref[:, local] = (made + rg_ref[:, there].astype(F32)).astype(BF16)
        target.send()
    gu_ref, ru_ref = gu.ready(), ru.ready()
    for target, side in ((us, 1 - own), (uk, own)):
        rows = block_at(side, quarter)
        for i in range(gu_ref.shape[1] // part):
            local = slice(i * part, i * part + part)
            made = matmul(n2t_ref[rows, :], gu_ref[:, local])
            target.ref[:, local] = (made + ru_ref[rows, local].astype(F32)).astype(BF16)
        target.send()


def attend_back_kernel(dproj_ref, probs_in, q, k, v, g, n1t, ct, att, gq, gk, gv, bias, sent,
                       probs_ref, probs_sem, gs_ref, gp_ref, acc_ref):
    def probs_copy(p):
        at = pl.ds(2 * p, 2)
        return pltpu.make_async_copy(probs_in.at[at], probs_ref.at[at], probs_sem.at[p])

    pairs = probs_ref.shape[0] // 2
    for p in range(pairs):
        probs_copy(p).start()
    q_ref, k_ref, v_ref, g_ref = q.ready(), k.ready(), v.ready(), g.ready()
    length = q_ref.shape[0]
    blocks = length // 128
    first = lax.broadcasted_iota(jnp.int32, (1, 128), 1) < 64
    acc_ref[:, :, (2 * blocks - 1) * 128 :] = jnp.zeros((2, 128, 128), F32)

    def pair(p, carry):
        own_lanes = block_at(p, 128)
        queries, keys = q_ref[:, own_lanes], k_ref[:, own_lanes]
        values, grads = v_ref[:, own_lanes], g_ref[:, own_lanes]
        grad_queries, grad_keys, grad_values = [], [], []
        probs_copy(p).wait()
        for head in range(2):
            own = jnp.where(first == (head == 0), grads, jnp.zeros_like(grads))
            gp_ref[head] = matmul(values, own, NT)
            for t in range(blocks):
                lanes = slice(128 * t, 128 * t + 128)
                inner = jnp.zeros((1, 128), F32)
                products = []
                for a in range(blocks):
                    rows = slice(128 * a, 128 * a + 128)
                    product = gp_ref[head, rows, lanes] * probs_ref[2 * p + head, rows, lanes].astype(F32)
                    inner = inner + product.sum(axis=0, keepdims=True)
                    products.append(product)
                for a in range(blocks):
                    rows = slice(128 * a, 128 * a + 128)
                    grad_scores = products[a] - probs_ref[2 * p + head, rows, lanes].astype(F32) * inner
                    gs_ref[head, rows, lanes] = grad_scores.astype(BF16)
                    start = length - 128 - 128 * a + 128 * t
                    if t == 0 or a == 0:
                        acc_ref[head, :, start : start + 128] = grad_scores
                    else:
                        acc_ref[head, :, start : start + 128] += grad_scores
            grad_values.append(matmul(probs_ref[2 * p + head], grads))
            grad_keys.append(matmul(gs_ref[head], queries))
            grad_queries.append(matmul(gs_ref[head], keys, TN))
            folded = acc_ref[head, 0:8, :]
            for c in range(1, 16):
                folded = folded + pltpu.roll(acc_ref[head, 8 * c : 8 * c + 8, :], 2 * length - 8 * c, 1)
            bias.ref[2 * p + head] = folded
        gq.ref[:, own_lanes] = jnp.where(first, grad_queries[0], grad_queries[1]).astype(BF16)
        gk.ref[:, own_lanes] = jnp.where(first, grad_keys[0], grad_keys[1]).astype(BF16)
        gv.ref[:, own_lanes] = jnp.where(first, grad_values[0], grad_values[1]).astype(BF16)
        return carry

    lax.fori_loop(0, pairs, pair, 0)
    for result in (gq, gk, gv, bias):
        result.send()
    half, model = sent.ref.shape[0], q_ref.shape[1]
    n1t_ref, ct_ref, att_ref = n1t.ready(), ct.ready(), att.ready()
    for place, (left, right) in enumerate(((n1t_ref, gq.ref), (n1t_ref, gk.ref), (n1t_ref, gv.ref), (ct_ref, att_ref))):
        sent.ref[:, place * model : (place + 1) * model] = matmul(left[...], right[...]).astype(BF16)
    sent.ref[:, 4 * model :] = dproj_ref[block_at(1 - bit_of_wide(0), half), :]


def heads_keep_kernel(dproj_ref, share1_ref, share2_ref, share3_ref, n1t, ct, gq, gk, gv, att, recv,
                      asent, akeep, bsent, bkeep, dgain):
    for i, share_ref in enumerate((share1_ref, share2_ref, share3_ref)):
        dgain.ref[i : i + 1, :] = jnp.sum(share_ref[...], axis=0, keepdims=True)
    half, model = asent.ref.shape
    quarter = bsent.ref.shape[0]
    own = bit_of_wide(1)
    n1t_ref, gq_ref, gk_ref, recv_ref = n1t.ready(), gq.ready(), gk.ready(), recv.ready()
    grad_query = (matmul(n1t_ref[...], gq_ref[...]) + recv_ref[:, :model].astype(F32)).astype(BF16)
    grad_key = (matmul(n1t_ref[...], gk_ref[...]) + recv_ref[:, model : 2 * model].astype(F32)).astype(BF16)
    first = lax.axis_index("stream") == 0
    asent.ref[...] = jnp.where(first, grad_key, grad_query)
    asent.send()
    akeep.ref[...] = jnp.where(first, grad_query, grad_key)
    akeep.send()
    ct_ref, gv_ref, att_ref = ct.ready(), gv.ready(), att.ready()
    for target, side in ((bsent, 1 - own), (bkeep, own)):
        rows = block_at(side, quarter)
        arrived = recv_ref[rows, 2 * model : 3 * model].astype(F32)
        target.ref[:, :model] = (matmul(n1t_ref[rows, :], gv_ref[...]) + arrived).astype(BF16)
        arrived = recv_ref[rows, 3 * model : 4 * model].astype(F32)
        target.ref[:, model : 2 * model] = (matmul(ct_ref[rows, :], att_ref[...]) + arrived).astype(BF16)
        arrived = recv_ref[rows, 4 * model :].astype(F32)
        mine = dproj_ref[block_at(2 * bit_of_wide(0) + side, quarter), :].astype(F32)
        target.ref[:, 2 * model :] = (mine + arrived).astype(BF16)
        target.send()


def start_back_kernel(gain_ref, gq, wq, gk, wk, gv, wv, x, gmid, tok, dgain):
    tok.ref[...] = matmul(gq.ready()[...], wq.ready()[...], NT)
    tok.ref[...] += matmul(gk.ready()[...], wk.ready()[...], NT)
    tok.ref[...] += matmul(gv.ready()[...], wv.ready()[...], NT)
    dgain.ref[...] = jnp.zeros_like(dgain.ref)
    x_ref, gmid_ref, gain = x.ready(), gmid.ready(), line_of(gain_ref)
    quarter = x_ref.shape[0] // 4

    def norm(rows):
        grad, shares = norm_back(x_ref[rows, :].astype(F32), gain, tok.ref[rows, :])
        tok.ref[rows, :] = gmid_ref[rows, :] + grad
        dgain.ref[...] += shares

    for i in range(2):
        norm(slice(2 * i * quarter, 2 * (i + 1) * quarter))
        tok.send((pl.ds(2 * i * quarter, 2 * quarter),))


def bias_grad_of(folded, buckets, length):
    heads = folded.shape[0]
    place = jnp.arange(2 * length, dtype=jnp.int32)[None, :] - jnp.arange(8, dtype=jnp.int32)[:, None]
    place = (place + 128) % (2 * length)
    onehot = bucket_of(length - place)[:, :, None] == jnp.arange(buckets, dtype=jnp.int32)
    return jnp.dot(
        folded.reshape(heads, -1), onehot.reshape(-1, buckets).astype(F32), precision=HIGHEST
    ).T


def match(query_emb, picked, mask, positive):
    inverse = 1.0 / math.sqrt(query_emb.shape[-1])
    scores = jnp.einsum("aip,bakp->abki", query_emb, picked, preferred_element_type=F32) * inverse
    best = jax.nn.logsumexp(scores, axis=2)
    values = mask.astype(F32)
    weight = values / jnp.maximum(jnp.sum(values, axis=-1, keepdims=True), 1.0)
    logits = jnp.sum(best * weight[:, None, :], axis=-1) / SOFTMAX_TEMP
    partition = jax.nn.logsumexp(logits, axis=1)
    target = (
        jnp.arange(logits.shape[1], dtype=jnp.int32)[None, :] == positive[:, None]
    ).astype(F32)
    losses = partition - jnp.sum(logits * target, axis=1)
    grad_scores = (jnp.exp(logits - partition[:, None]) - target) / SOFTMAX_TEMP
    soft = jnp.exp(scores - best[:, :, None, :])
    grad_tokens = (grad_scores[:, :, None, None] * weight[:, None, None, :] * soft).astype(BF16)
    own = jnp.einsum("abki,bakp->aip", grad_tokens, picked, preferred_element_type=F32) * inverse
    picks = jnp.einsum("abki,aip->bakp", grad_tokens, query_emb, preferred_element_type=F32) * inverse
    return losses, own.astype(BF16), picks.astype(BF16)


def per_device(
    tokens,
    doc_segments,
    query_mask,
    positives,
    top_index,
    query_weight,
    key_weight,
    value_weight,
    output_weight,
    gate_weight,
    up_weight,
    down_weight,
    projection,
    attention_gain,
    feedforward_gain,
    final_gain,
    bias_table,
):
    length, model = tokens.shape[2], tokens.shape[3]
    heads = bias_table.shape[1]
    query_len = query_mask.shape[1]
    embed = projection.shape[1]
    hidden_width = gate_weight.shape[1]
    top = top_index.shape[2]
    width = lax.axis_size("wide")
    bits = width.bit_length() - 1
    row_queries = length // query_len
    half = row_queries // 2
    stream = lax.axis_index("stream")
    place = lax.axis_index("wide")
    is_query = stream == 0
    gain1, gain2, gain3 = (Small(g.reshape(-1, 128)) for g in (attention_gain, feedforward_gain, final_gain))
    part = 512
    order = tuple(range(bits))
    down_order = (0, 2, 1) + order[3:]

    inputs = tokens.reshape(length, model)
    flat = shape_of(length, model)
    flat32 = shape_of(length, model, dtype=F32)
    wide_flat = shape_of(length, hidden_width)
    shares = shape_of(8, model, dtype=F32)
    square = pltpu.VMEM((length, length), F32)
    pair_sems = pltpu.SemaphoreType.DMA((heads // 2,))
    all_probs = pltpu.VMEM((heads, length, length), BF16)
    picks = top_index.reshape(width, 2, half, top).transpose(1, 0, 2, 3).reshape(-1, 128)
    (
        normed_one, queries, keys, values, context, probs, middle, normed_two, up_factor, gate_factor, hidden, block_out,
        normed_three, lower, upper, picked,
    ) = call(
        partial(forward_kernel, query_len, part),
        [flat] * 5 + [shape_of(heads, length, length), flat32, flat, wide_flat, wide_flat, wide_flat, flat32, flat,
         shape_of(length // 2, embed), shape_of(length // 2, embed), shape_of(picks.size, embed)],
        scratch=[
            square, pltpu.VMEM((heads, 1, 2 * length), F32), pltpu.VMEM((2, 128, 2 * length), F32),
            pltpu.VMEM((2, length, length), F32), all_probs,
            pair_sems, pltpu.VMEM((length, part), F32), pltpu.VMEM((length, part), F32), pltpu.VMEM((length, embed), BF16),
        ],
        name="forward", us=25, raw_results=(5,),
    )(
        bias_table.T, Small(doc_segments), gain1, gain2, gain3, Small(picks), inputs, query_weight, key_weight,
        value_weight, output_weight, gate_weight, up_weight, down_weight, projection,
    )

    other_half = flip_stream(upper)
    both = ("stream", "wide")
    gathered = lax.all_to_all(picked.reshape(2 * width, half * top, embed), both, 0, 0, tiled=True)
    query_emb = jnp.where(is_query, lower, other_half)
    start = place * row_queries + stream * half
    losses, own_grads, pick_grads = match(
        query_emb.reshape(half, query_len, embed),
        gathered[width:].reshape(width, half, top, embed),
        lax.dynamic_slice_in_dim(query_mask, start, half, 0),
        lax.dynamic_slice_in_dim(positives, start, half, 0),
    )
    pick_grads = pick_grads.reshape(width, half * top, embed)
    returned = lax.all_to_all(
        jnp.concatenate([jnp.zeros_like(pick_grads), pick_grads], axis=0), both, 0, 0, tiled=True
    )
    loss_high = losses.astype(BF16)
    loss_low = (losses - loss_high.astype(F32)).astype(BF16)
    other_loss = flip_stream(jnp.stack([loss_high, loss_low])).astype(F32)
    other_loss = other_loss[0] + other_loss[1]
    query_loss = jnp.where(
        is_query,
        jnp.concatenate([losses, other_loss]),
        jnp.concatenate([other_loss, losses]),
    )
    own_grads = own_grads.reshape(length // 2, embed)
    other_grads = flip_stream(own_grads)

    source = blocks_ordered(jnp.arange(model, dtype=jnp.int32), width, order).reshape(1, model)
    tall = shape_of(model, length)
    n1_t, n2_t, n3_t, context_t, onehot = call(
        turn_kernel, [tall] * 4 + [shape_of(length, picks.size)], scratch=[pltpu.VMEM((model, model), BF16)], name="turn", us=4
    )(Small(source), Small(picks), normed_one, normed_two, normed_three, context)
    hidden_t = blocks_ordered(hidden.T, width, down_order)

    def core():
        return bit_of_wide(0)

    def other_core():
        return 1 - bit_of_wide(0)

    many = picks.size > 2048
    onehot_operand = Raw(onehot) if many else onehot
    pieces_of_picks = [pltpu.VMEM((length, 2048), BF16), pltpu.SemaphoreType.DMA] if many else []
    half_rows = shape_of(model // 2, hidden_width)
    (
        down_send, branch, grad_gate, grad_up, gate_send, up_send, grad_projection, grad_middle, attended,
        grad_context, shares2, shares3,
    ) = call(
        partial(upper_back_kernel, part),
        [shape_of(hidden_width // 2, model), flat, wide_flat, wide_flat, half_rows,
         half_rows, shape_of(model, embed), flat32, flat, flat, shares,
         shares],
        scratch=[
            pltpu.VMEM((length, embed), BF16), pltpu.VMEM((length, model), F32), pltpu.VMEM((length, part), F32),
            pltpu.VMEM((length, embed), F32),
        ]
        + pieces_of_picks,
        name="upper_back", us=18, after=(other_loss,), pieces={9: (0, 4), 10: (1, 4), 11: (1, 4)},
    )(
        Small(projection), gain2, gain3, own_grads, other_grads, returned.reshape(-1, embed), onehot_operand, block_out,
        Part(hidden_t, other_core, hidden_width // 2), down_weight, up_factor, gate_factor,
        Part(n2_t, other_core, model // 2), n3_t, gate_weight, up_weight, middle, output_weight,
    )
    down_recv = flip_wide(down_send, 0)
    gate_recv = flip_wide(gate_send, 0)
    up_recv = flip_wide(up_send, 0)

    down_send, down_keep = call(
        down_keep_kernel, [shape_of(hidden_width // 4, model)] * 2, name="down_keep", us=4
    )(branch, Part(hidden_t, core, hidden_width // 2), down_recv)
    down_recv = flip_wide(down_send, 2)

    gate_send, gate_keep, up_send, up_keep = call(
        partial(gates_keep_kernel, part),
        [shape_of(model // 2, hidden_width // 2)] * 2 + [shape_of(model // 4, hidden_width)] * 2,
        name="gates_keep", us=6, after=(down_keep,),
    )(Part(n2_t, core, model // 2), grad_gate, gate_recv, grad_up, up_recv)
    gate_recv = flip_stream(gate_send)
    up_recv = flip_wide(up_send, 1)

    widest = 4 * model + embed
    grad_queries, grad_keys, grad_values, folded, heads_send = call(
        attend_back_kernel,
        [flat, flat, flat, shape_of(heads, 8, 2 * length, dtype=F32), shape_of(model // 2, widest)],
        scratch=[
            all_probs, pair_sems, pltpu.VMEM((2, length, length), BF16), pltpu.VMEM((2, length, length), F32),
            pltpu.VMEM((2, 128, 2 * length), F32),
        ],
        name="attend_back", us=14, after=(up_keep,),
    )(
        Small(grad_projection), Raw(probs), queries, keys, values, grad_context, Part(n1_t, other_core, model // 2),
        Part(context_t, other_core, model // 2), attended,
    )
    down_sum = halve_rows(added(down_keep, down_recv), 1)
    heads_recv = flip_wide(heads_send, 0)
    gate_sum = added(gate_keep, gate_recv)
    up_sum = added(up_keep, up_recv)
    grad_tokens, shares1 = call(
        start_back_kernel, [flat32, shares], name="start_back", us=5, after=(heads_send, down_sum, gate_recv, up_recv)
    )(gain1, grad_queries, query_weight, grad_keys, key_weight, grad_values, value_weight, inputs, grad_middle)
    a_send, a_keep, b_send, b_keep, gain_grads = call(
        heads_keep_kernel,
        [shape_of(model // 2, model)] * 2 + [shape_of(model // 4, 2 * model + embed)] * 2
        + [shape_of(3, model, dtype=F32)],
        name="heads_keep", us=4, after=(grad_tokens,),
    )(
        Small(grad_projection), Small(shares1), Small(shares2), Small(shares3), Part(n1_t, core, model // 2),
        Part(context_t, core, model // 2), grad_queries, grad_keys, grad_values, attended, heads_recv,
    )
    a_sum = added(a_keep, flip_stream(a_send))
    b_sum = added(b_keep, flip_wide(b_send, 1))

    for bit in down_order[3:]:
        down_sum = halve_rows(down_sum, bit)
    down_sum = down_sum.astype(F32) + flip_stream(down_sum).astype(F32)

    def finish(first, second):
        block = jnp.concatenate([halve_rows(first, 1), second], axis=1)
        for bit in range(2, bits):
            block = halve_rows(block, bit)
        other = flip_stream(block)
        edge = first.shape[1]
        mine, theirs = block[:, :edge].astype(F32), other[:, :edge].astype(F32)
        left, right = jnp.where(is_query, mine, theirs), jnp.where(is_query, theirs, mine)
        return left, right, block[:, edge:].astype(F32) + other[:, edge:].astype(F32)

    gate_left, gate_right, sum_up = finish(gate_sum, up_sum)
    sum_query, sum_key, rest = finish(a_sum, b_sum)
    grad_table = bias_grad_of(folded, bias_table.shape[0], length)
    small = jnp.concatenate([gain_grads.reshape(-1), grad_table.reshape(-1)])
    small = sum_everywhere(small.reshape(-1, 128), width).reshape(-1)
    own_rows = model // width
    grad_gains = [lax.dynamic_slice_in_dim(small, i * model + place * own_rows, own_rows, 0) for i in range(3)]
    return (
        query_loss,
        grad_tokens.reshape(tokens.shape),
        sum_query,
        sum_key,
        rest[:, :model],
        rest[:, model : 2 * model],
        jnp.concatenate([gate_left, gate_right], axis=1),
        sum_up,
        down_sum,
        rest[:, 2 * model :],
        grad_gains[0],
        grad_gains[1],
        grad_gains[2],
        small[3 * model :].reshape(bias_table.shape),
    )


def solution(mesh):
    rows = P("wide", None)
    in_specs = (
        P("stream", "wide", None, None),
        rows,
        P(),
        P(),
        P(None, "wide", None),
    ) + (P(),) * 12
    out_specs = (P("wide"), P("stream", "wide", None, None)) + (rows,) * 8 + (P("wide"),) * 3 + (P(),)
    return jax.shard_map(
        per_device, mesh=mesh, in_specs=in_specs, out_specs=out_specs, check_vma=False
    )
```

```python
from functools import partial
import math

import jax
import jax.numpy as jnp
import numpy as np
from jax import lax
from jax.experimental import pallas as pl
from jax.experimental.pallas import tpu as pltpu
from jax.sharding import PartitionSpec as P

EPSILON = 1e-06
SOFTMAX_TEMP = 0.05
MASKED_SCORE = -1e30
HIGHEST = lax.Precision.HIGHEST
BF16 = jnp.bfloat16
F32 = jnp.float32
NT = (((1,), (1,)), ((), ()))
TN = (((0,), (0,)), ((), ()))


def matmul(left, right, dims=(((1,), (0,)), ((), ()))):
    return lax.dot_general(left, right, dims, preferred_element_type=F32)


def flip_stream(block):
    return lax.ppermute(block, "stream", [(0, 1), (1, 0)])


def flip_wide(block, bit):
    devices = range(lax.axis_size("wide"))
    return lax.ppermute(block, "wide", [(i, i ^ (1 << bit)) for i in devices])


def added(kept, received):
    return (kept.astype(F32) + received.astype(F32)).astype(BF16)


def blocks_ordered(rows, width, order):
    bits = width.bit_length() - 1
    shaped = rows.reshape((2,) * bits + (rows.shape[0] // width,) + rows.shape[1:])
    axes = tuple(bits - 1 - bit for bit in order) + tuple(range(bits, shaped.ndim))
    return shaped.transpose(axes).reshape(rows.shape)


def halve_rows(block, bit):
    own = (lax.axis_index("wide") >> bit) & 1
    half = block.shape[0] // 2
    sent = lax.dynamic_slice_in_dim(block, (1 - own) * half, half, 0)
    kept = lax.dynamic_slice_in_dim(block, own * half, half, 0)
    return added(kept, flip_wide(sent, bit))


def sum_everywhere(block, width):
    block = block + flip_stream(block)
    for bit in range(width.bit_length() - 1):
        block = block + flip_wide(block, bit)
    return block


class Small:
    def __init__(self, array):
        self.array = array


class Raw:
    def __init__(self, array):
        self.array = array


class Part:
    def __init__(self, array, number, size):
        self.array, self.number, self.size = array, number, size


class Fetched:
    def __init__(self, source, target, semaphores, axis, pieces):
        size = target.shape[axis] // pieces
        at = [(slice(None),) * axis + (pl.ds(i * size, size),) for i in range(pieces)]
        self.target = target
        self.copies = [
            pltpu.make_async_copy(source.at[at[i]], target.at[at[i]], semaphores[i]) for i in range(pieces)
        ]
        for copy in self.copies:
            copy.start()

    def piece(self, i):
        if self.copies[i] is not None:
            self.copies[i].wait()
            self.copies[i] = None
        return self.target

    def ready(self):
        for i in range(len(self.copies)):
            self.piece(i)
        return self.target


class Result:
    def __init__(self, ref, target, semaphores):
        self.ref, self.target, self.semaphores = ref, target, semaphores
        self.copies = []

    def send(self, at=(slice(None),)):
        copy = pltpu.make_async_copy(self.ref.at[at], self.target.at[at], self.semaphores[len(self.copies)])
        copy.start()
        self.copies.append(copy)


def call(kernel, out_shape, scratch=(), name=None, after=(), us=5, pieces=None, raw_results=(), limit=56):
    pieces = pieces or {}

    def built(*operands):
        taken, results = len(operands), len(out_shape)
        arrays, buffers, semaphores = [], [], 0
        for i, operand in enumerate(operands):
            wrapped = isinstance(operand, Small | Raw | Part)
            array = operand.array if wrapped else operand
            arrays.append(array if isinstance(operand, Small) else pltpu.with_memory_space_constraint(array, pltpu.HBM))
            if not isinstance(operand, Small | Raw):
                rows = operand.size if isinstance(operand, Part) else array.shape[0]
                buffers.append(pltpu.VMEM((rows,) + array.shape[1:], array.dtype))
                semaphores += pieces.get(i, (0, 1))[1]
        fetched = len(buffers)
        send_at = semaphores
        for i, out in enumerate(out_shape):
            if i not in raw_results:
                buffers.append(pltpu.VMEM(out.shape, out.dtype))
                semaphores += 4

        def run(*refs):
            outputs = refs[taken + len(after) : taken + len(after) + results]
            rest = refs[taken + len(after) + results :]
            slots, sems, own = rest[: len(buffers)], rest[len(buffers)], rest[len(buffers) + 1 :]
            given, place, at = [], 0, 0
            for i, operand in enumerate(operands):
                if isinstance(operand, Small | Raw):
                    given.append(refs[i])
                    continue
                source = refs[i]
                if isinstance(operand, Part):
                    source = source.at[block_at(operand.number(), operand.size)]
                axis, count = pieces.get(i, (0, 1))
                given.append(Fetched(source, slots[place], [sems.at[at + j] for j in range(count)], axis, count))
                place, at = place + 1, at + count
            made, at = [], send_at
            for i, output in enumerate(outputs):
                if i in raw_results:
                    made.append(output)
                    continue
                made.append(Result(slots[place], output, [sems.at[at + j] for j in range(4)]))
                place, at = place + 1, at + 4
            kernel(*given, *made, *own)
            for operand in given:
                if isinstance(operand, Fetched):
                    operand.ready()
            for i, result in enumerate(made):
                if i not in raw_results:
                    if not result.copies:
                        result.send()
                    for copy in result.copies:
                        copy.wait()

        return pl.pallas_call(
            run,
            in_specs=[pl.BlockSpec(memory_space=pltpu.VMEM if isinstance(x, Small) else pl.ANY) for x in operands]
            + [pl.BlockSpec(memory_space=pl.ANY)] * len(after),
            out_specs=[pl.BlockSpec(memory_space=pl.ANY)] * results,
            out_shape=[pltpu.HBM(x.shape, x.dtype) for x in out_shape],
            scratch_shapes=buffers + [pltpu.SemaphoreType.DMA((max(semaphores, 1),))] + list(scratch),
            compiler_params=pltpu.CompilerParams(vmem_limit_bytes=limit << 20),
            cost_estimate=pl.CostEstimate(flops=0, bytes_accessed=int(us * 3.3e6), transcendentals=0),
            name=name,
        )(*arrays, *after)

    return built


def shape_of(*shape, dtype=BF16):
    return jax.ShapeDtypeStruct(shape, dtype)


def tiles(total, size, body):
    def step(i, carry):
        body(pl.ds(pl.multiple_of(i * size, size), size))
        return carry

    lax.fori_loop(0, total // size, step, 0, unroll=2)


def block_at(index, size):
    return pl.ds(pl.multiple_of(index * size, size), size)


def bit_of_wide(bit):
    return (lax.axis_index("wide") >> bit) & 1


def normed(values, gain):
    inverse = lax.rsqrt(jnp.mean(values * values, axis=-1, keepdims=True) + EPSILON)
    return values * inverse * gain


def norm_back(values, gain, upstream):
    inverse = lax.rsqrt(jnp.mean(values * values, axis=-1, keepdims=True) + EPSILON)
    unit = values * inverse
    weighted = upstream * gain
    inner = jnp.mean(weighted * unit, axis=-1, keepdims=True)
    shares = (upstream * unit).reshape(-1, 8, values.shape[1]).sum(axis=0)
    return (weighted - unit * inner) * inverse, shares


def bucket_of(offset):
    distance = jnp.abs(offset)
    far_bucket = jnp.full(offset.shape, 8, jnp.int32)
    for exponent in range(1, 8):
        far_bucket = far_bucket + (distance * distance >= 64 * 2**exponent).astype(jnp.int32)
    near_bucket = jnp.where(distance < 8, distance, far_bucket)
    return near_bucket + 16 * (offset > 0).astype(jnp.int32)


def line_of(gain_ref):
    return jnp.concatenate([gain_ref[i : i + 1, :] for i in range(gain_ref.shape[0])], axis=1)


def forward_kernel(query_len, part, table, seg_ref, gain1_ref, gain2_ref, gain3_ref, picks_ref, x, wq, wk, wv, wo, wg, wu,
                   wd, proj, n1, q, k, v, ctx, probs_out, mid, n2, up_factor, gate_factor, hidden, out, n3, lower, upper, picked,
                   mask_ref, line_ref, base_ref, score_ref, probs_ref, probs_sem, gate_ref, up_ref, emb_ref):
    x_ref = x.ready()
    length, model = x_ref.shape
    blocks = length // 128
    table_ref = table.target
    heads = table_ref.shape[0]
    gain = line_of(gain1_ref)

    def norm(rows):
        n1.ref[rows, :] = normed(x_ref[rows, :].astype(F32), gain).astype(BF16)

    tiles(length, 256, norm)
    n1.send()
    for result, weight in ((q, wq), (k, wk), (v, wv)):
        result.ref[...] = matmul(n1.ref[...], weight.ready()[...]).astype(BF16)
        result.send()

    lane = lax.broadcasted_iota(jnp.int32, (1, length), 1)
    segments = jnp.where(lax.axis_index("stream") == 0, lane // query_len, seg_ref[...])
    for a in range(blocks):
        column = jnp.broadcast_to(segments[:, 128 * a : 128 * a + 128], (128, 128)).T[:, 0:1]
        mask_ref[128 * a : 128 * a + 128, :] = jnp.where(column == segments, 0.0, MASKED_SCORE)
    offsets = length - lax.broadcasted_iota(jnp.int32, (1, 2 * length), 1)
    buckets = lax.broadcasted_iota(jnp.int32, (table_ref.shape[1], 2 * length), 0)
    onehot = jnp.where(bucket_of(offsets) == buckets, 1.0, 0.0)
    lines = jnp.dot(table.ready()[...], onehot, precision=HIGHEST, preferred_element_type=F32)
    for head in range(heads):
        line_ref[head] = lines[head : head + 1, :]
    first = lax.broadcasted_iota(jnp.int32, (1, 128), 1) < 64

    def probs_copy(p):
        at = pl.ds(2 * p, 2)
        return pltpu.make_async_copy(probs_ref.at[at], probs_out.at[at], probs_sem.at[p])

    def pair(p, carry):
        own_lanes = block_at(p, 128)
        queries, keys, values = q.ref[:, own_lanes], k.ref[:, own_lanes], v.ref[:, own_lanes]
        contexts = []
        for head in range(2):
            line = jnp.broadcast_to(line_ref[2 * p + head], (128, 2 * length))
            base_ref[head] = pltpu.roll(line, 2 * length - 128, 1, stride=1, stride_axis=0)
            own = jnp.where(first == (head == 0), queries, jnp.zeros_like(queries))
            score_ref[head] = matmul(keys, own, NT)
            for t in range(blocks):
                lanes = slice(128 * t, 128 * t + 128)
                scores = []
                for a in range(blocks):
                    rows = slice(128 * a, 128 * a + 128)
                    start = length - 128 - 128 * a + 128 * t
                    scores.append(score_ref[head, rows, lanes] + base_ref[head, :, start : start + 128] + mask_ref[rows, lanes])
                top = scores[0].max(axis=0, keepdims=True)
                for block in scores[1:]:
                    top = jnp.maximum(top, block.max(axis=0, keepdims=True))
                total = jnp.zeros_like(top)
                for a in range(blocks):
                    scores[a] = jnp.exp(scores[a] - top)
                    total = total + scores[a].sum(axis=0, keepdims=True)
                inverse = 1.0 / total
                for a in range(blocks):
                    probs_ref[2 * p + head, 128 * a : 128 * a + 128, lanes] = (scores[a] * inverse).astype(BF16)
            contexts.append(matmul(probs_ref[2 * p + head], values, TN))
        ctx.ref[:, own_lanes] = jnp.where(first, contexts[0], contexts[1]).astype(BF16)
        probs_copy(p).start()
        return carry

    lax.fori_loop(0, heads // 2, pair, 0, unroll=3)
    ctx.send()
    mid.ref[...] = matmul(ctx.ref[...], wo.ready()[...])
    gain = line_of(gain2_ref)

    def start(rows):
        middle = x_ref[rows, :].astype(F32) + mid.ref[rows, :]
        mid.ref[rows, :] = middle
        n2.ref[rows, :] = normed(middle, gain).astype(BF16)

    tiles(length, 256, start)
    mid.send()
    n2.send()
    scale = math.sqrt(2.0 / math.pi)
    wg_ref, wu_ref = wg.ready(), wu.ready()

    def column(columns):
        gate_ref[...] = matmul(n2.ref[...], wg_ref[:, columns])
        up_ref[...] = matmul(n2.ref[...], wu_ref[:, columns])

        def gelu(rows):
            u, up = gate_ref[rows, :], up_ref[rows, :]
            squared = u * u
            tanh = jnp.tanh(scale * u * (1.0 + 0.044715 * squared))
            gate = 0.5 * (1.0 + tanh)
            slope = gate + 0.5 * u * (1.0 - tanh * tanh) * (scale * (1.0 + 3 * 0.044715 * squared))
            value = u * gate
            up_factor.ref[rows, columns] = value.astype(BF16)
            gate_factor.ref[rows, columns] = (up * slope).astype(BF16)
            hidden.ref[rows, columns] = (value * up).astype(BF16)

        tiles(length, 32, gelu)

    tiles(wg_ref.shape[1], part, column)
    for result in (hidden, up_factor, gate_factor):
        result.send()
    out.ref[...] = matmul(hidden.ref[...], wd.ready()[...])
    gain = line_of(gain3_ref)

    def end(rows):
        value = out.ref[rows, :] + mid.ref[rows, :]
        out.ref[rows, :] = value
        n3.ref[rows, :] = normed(value, gain).astype(BF16)

    tiles(length, 256, end)
    out.send()
    n3.send()
    emb_ref[...] = matmul(n3.ref[...], proj.ready()[...]).astype(BF16)
    lower.ref[...] = emb_ref[: length // 2, :]
    upper.ref[...] = emb_ref[length // 2 :, :]
    lower.send()
    upper.send()
    tokens = lax.broadcasted_iota(jnp.int32, (1, 128), 1)

    def pick(i, carry):
        column = jnp.broadcast_to(picks_ref[pl.ds(i, 1), :], (128, 128)).T
        onehot = jnp.concatenate(
            [jnp.where(column == tokens + 128 * t, 1.0, 0.0).astype(BF16) for t in range(blocks)], axis=1
        )
        picked.ref[block_at(i, 128), :] = matmul(onehot, emb_ref[...]).astype(BF16)
        return carry

    lax.fori_loop(0, picks_ref.shape[0], pick, 0, unroll=8 if picks_ref.shape[0] % 8 == 0 else 1)
    picked.send()
    for p in range(heads // 2):
        probs_copy(p).wait()


def turn_kernel(source_ref, picks_ref, *refs):
    onehot, refs = refs[-2], refs[:-2] + refs[-1:]
    count = (len(refs) - 1) // 2
    tokens = lax.broadcasted_iota(jnp.int32, (onehot.ref.shape[0], 128), 0)

    def pick(i, carry):
        onehot.ref[:, block_at(i, 128)] = jnp.where(picks_ref[pl.ds(i, 1), :] == tokens, 1.0, 0.0).astype(BF16)
        return carry

    lax.fori_loop(0, picks_ref.shape[0], pick, 0)
    onehot.send()
    order_ref = refs[-1]
    size = source_ref.shape[1]
    for i in range(size // 128):
        column = jnp.broadcast_to(source_ref[:, 128 * i : 128 * i + 128], (128, 128)).T
        for j in range(size // 128):
            lane = lax.broadcasted_iota(jnp.int32, (1, 128), 1) + 128 * j
            order_ref[128 * i : 128 * i + 128, 128 * j : 128 * j + 128] = jnp.where(column == lane, 1.0, 0.0).astype(BF16)
    for taken, made in zip(refs[:count], refs[count : 2 * count]):
        made.ref[...] = matmul(order_ref[...], taken.ready()[...], NT).astype(BF16)
        made.send()


def upper_back_kernel(part, proj_ref, gain2_ref, gain3_ref, own, other, returned, onehot, block, ht, wd, upf, gatef,
                      n2t, n3t, wg, wu, mid, wo, dsent, branch, gg, gu, sg, su, dproj, gmid, att, gctx, dgain2, dgain3,
                      emb_ref, gout_ref, grad_ref, doc_ref, piece_ref=None, piece_sem=None):
    length = gmid.ref.shape[0]
    half = length // 2
    is_query = lax.axis_index("stream") == 0
    returned_ref = returned.ready()
    if isinstance(onehot, Fetched):
        doc_ref[...] = matmul(onehot.ready()[...], returned_ref[...])
    else:
        size = piece_ref.shape[1]
        doc_ref[...] = jnp.zeros_like(doc_ref)

        def add(i, carry):
            copy = pltpu.make_async_copy(onehot.at[:, block_at(i, size)], piece_ref, piece_sem)
            copy.start()
            copy.wait()
            doc_ref[...] += matmul(piece_ref[...], returned_ref[block_at(i, size), :])
            return carry

        lax.fori_loop(0, returned_ref.shape[0] // size, add, 0)
    for side, query in enumerate((own, other)):
        rows = slice(side * half, side * half + half)
        emb_ref[rows, :] = jnp.where(is_query, query.ready()[...], doc_ref[rows, :].astype(BF16))
    gout_ref[...] = matmul(emb_ref[...], proj_ref[...], NT)
    dgain2.ref[...] = jnp.zeros_like(dgain2.ref)
    dgain3.ref[...] = jnp.zeros_like(dgain3.ref)
    block_ref, gain3 = block.ready(), line_of(gain3_ref)

    def norm3(rows):
        grad, shares = norm_back(block_ref[rows, :], gain3, gout_ref[rows, :])
        dgain3.ref[...] += shares
        gout_ref[rows, :] = grad
        branch.ref[rows, :] = grad.astype(BF16)

    tiles(length, 256, norm3)
    branch.send()
    dsent.ref[...] = matmul(ht.ready()[...], branch.ref[...]).astype(BF16)
    dsent.send()

    for i in range(gg.ref.shape[1] // part):
        columns = slice(i * part, i * part + part)
        grad_ref[...] = matmul(branch.ref[...], wd.piece(i)[columns, :], NT)
        upf_ref, gatef_ref = upf.piece(i), gatef.piece(i)

        def factors(rows):
            grad = grad_ref[rows, :]
            gu.ref[rows, columns] = (grad * upf_ref[rows, columns].astype(F32)).astype(BF16)
            gg.ref[rows, columns] = (grad * gatef_ref[rows, columns].astype(F32)).astype(BF16)

        tiles(length, 64, factors)
    n2t_ref = n2t.ready()
    sg.ref[...] = matmul(n2t_ref[...], gg.ref[...]).astype(BF16)
    su.ref[...] = matmul(n2t_ref[...], gu.ref[...]).astype(BF16)
    gg.send()
    gu.send()
    sg.send()
    dproj.ref[...] = matmul(n3t.ready()[...], emb_ref[...]).astype(BF16)
    dproj.send()
    su.send()

    gmid.ref[...] = matmul(gg.ref[...], wg.ready()[...], NT)
    gmid.ref[...] += matmul(gu.ref[...], wu.ready()[...], NT)
    mid_ref, gain2 = mid.ready(), line_of(gain2_ref)

    def norm2(rows):
        grad, shares = norm_back(mid_ref[rows, :], gain2, gmid.ref[rows, :])
        grad = grad + gout_ref[rows, :]
        dgain2.ref[...] += shares
        gmid.ref[rows, :] = grad
        att.ref[rows, :] = grad.astype(BF16)

    tiles(length, 256, norm2)
    gmid.send()
    att.send()
    gctx.ref[...] = matmul(att.ref[...], wo.ready()[...], NT).astype(BF16)


def down_keep_kernel(branch, ht, recv, sent, keep):
    half = sent.ref.shape[0]
    own = bit_of_wide(2)
    branch_ref, ht_ref, recv_ref = branch.ready(), ht.ready(), recv.ready()
    for target, side in ((sent, 1 - own), (keep, own)):
        rows = block_at(side, half)
        target.ref[...] = (matmul(ht_ref[rows, :], branch_ref[...]) + recv_ref[rows, :].astype(F32)).astype(BF16)
        target.send()


def gates_keep_kernel(part, n2t, gg, rg, gu, ru, gs, gk, us, uk):
    columns = gs.ref.shape[1]
    quarter = us.ref.shape[0]
    own, stream = bit_of_wide(1), lax.axis_index("stream")
    n2t_ref, gg_ref, rg_ref = n2t.ready(), gg.ready(), rg.ready()
    for target, side in ((gs, 1 - stream), (gk, stream)):
        for i in range(columns // part):
            local = slice(i * part, i * part + part)
            there = block_at(side * (columns // part) + i, part)
            made = matmul(n2t_ref[...], gg_ref[:, there])
            target.ref[:, local] = (made + rg_ref[:, there].astype(F32)).astype(BF16)
        target.send()
    gu_ref, ru_ref = gu.ready(), ru.ready()
    for target, side in ((us, 1 - own), (uk, own)):
        rows = block_at(side, quarter)
        for i in range(gu_ref.shape[1] // part):
            local = slice(i * part, i * part + part)
            made = matmul(n2t_ref[rows, :], gu_ref[:, local])
            target.ref[:, local] = (made + ru_ref[rows, local].astype(F32)).astype(BF16)
        target.send()


def attend_back_kernel(dproj_ref, probs_in, q, k, v, g, n1t, ct, att, gq, gk, gv, bias, sent,
                       probs_ref, probs_sem, gs_ref, gp_ref, acc_ref):
    def probs_copy(p):
        at = pl.ds(2 * p, 2)
        return pltpu.make_async_copy(probs_in.at[at], probs_ref.at[at], probs_sem.at[p])

    pairs = probs_ref.shape[0] // 2
    for p in range(pairs):
        probs_copy(p).start()
    q_ref, k_ref, v_ref, g_ref = q.ready(), k.ready(), v.ready(), g.ready()
    length = q_ref.shape[0]
    blocks = length // 128
    first = lax.broadcasted_iota(jnp.int32, (1, 128), 1) < 64
    acc_ref[:, :, (2 * blocks - 1) * 128 :] = jnp.zeros((2, 128, 128), F32)

    def pair(p, carry):
        own_lanes = block_at(p, 128)
        queries, keys = q_ref[:, own_lanes], k_ref[:, own_lanes]
        values, grads = v_ref[:, own_lanes], g_ref[:, own_lanes]
        grad_queries, grad_keys, grad_values = [], [], []
        probs_copy(p).wait()
        for head in range(2):
            own = jnp.where(first == (head == 0), grads, jnp.zeros_like(grads))
            gp_ref[head] = matmul(values, own, NT)
            for t in range(blocks):
                lanes = slice(128 * t, 128 * t + 128)
                inner = jnp.zeros((1, 128), F32)
                products = []
                for a in range(blocks):
                    rows = slice(128 * a, 128 * a + 128)
                    product = gp_ref[head, rows, lanes] * probs_ref[2 * p + head, rows, lanes].astype(F32)
                    inner = inner + product.sum(axis=0, keepdims=True)
                    products.append(product)
                for a in range(blocks):
                    rows = slice(128 * a, 128 * a + 128)
                    grad_scores = products[a] - probs_ref[2 * p + head, rows, lanes].astype(F32) * inner
                    gs_ref[head, rows, lanes] = grad_scores.astype(BF16)
                    start = length - 128 - 128 * a + 128 * t
                    if t == 0 or a == 0:
                        acc_ref[head, :, start : start + 128] = grad_scores
                    else:
                        acc_ref[head, :, start : start + 128] += grad_scores
            grad_values.append(matmul(probs_ref[2 * p + head], grads))
            grad_keys.append(matmul(gs_ref[head], queries))
            grad_queries.append(matmul(gs_ref[head], keys, TN))
            folded = acc_ref[head, 0:8, :]
            for c in range(1, 16):
                folded = folded + pltpu.roll(acc_ref[head, 8 * c : 8 * c + 8, :], 2 * length - 8 * c, 1)
            bias.ref[2 * p + head] = folded
        gq.ref[:, own_lanes] = jnp.where(first, grad_queries[0], grad_queries[1]).astype(BF16)
        gk.ref[:, own_lanes] = jnp.where(first, grad_keys[0], grad_keys[1]).astype(BF16)
        gv.ref[:, own_lanes] = jnp.where(first, grad_values[0], grad_values[1]).astype(BF16)
        return carry

    lax.fori_loop(0, pairs, pair, 0)
    for result in (gq, gk, gv, bias):
        result.send()
    half, model = sent.ref.shape[0], q_ref.shape[1]
    n1t_ref, ct_ref, att_ref = n1t.ready(), ct.ready(), att.ready()
    for place, (left, right) in enumerate(((n1t_ref, gq.ref), (n1t_ref, gk.ref), (n1t_ref, gv.ref), (ct_ref, att_ref))):
        sent.ref[:, place * model : (place + 1) * model] = matmul(left[...], right[...]).astype(BF16)
    sent.ref[:, 4 * model :] = dproj_ref[block_at(1 - bit_of_wide(0), half), :]


def heads_keep_kernel(dproj_ref, share1_ref, share2_ref, share3_ref, n1t, ct, gq, gk, gv, att, recv,
                      asent, akeep, bsent, bkeep, dgain):
    for i, share_ref in enumerate((share1_ref, share2_ref, share3_ref)):
        dgain.ref[i : i + 1, :] = jnp.sum(share_ref[...], axis=0, keepdims=True)
    half, model = asent.ref.shape
    quarter = bsent.ref.shape[0]
    own = bit_of_wide(1)
    n1t_ref, gq_ref, gk_ref, recv_ref = n1t.ready(), gq.ready(), gk.ready(), recv.ready()
    grad_query = (matmul(n1t_ref[...], gq_ref[...]) + recv_ref[:, :model].astype(F32)).astype(BF16)
    grad_key = (matmul(n1t_ref[...], gk_ref[...]) + recv_ref[:, model : 2 * model].astype(F32)).astype(BF16)
    first = lax.axis_index("stream") == 0
    asent.ref[...] = jnp.where(first, grad_key, grad_query)
    asent.send()
    akeep.ref[...] = jnp.where(first, grad_query, grad_key)
    akeep.send()
    ct_ref, gv_ref, att_ref = ct.ready(), gv.ready(), att.ready()
    for target, side in ((bsent, 1 - own), (bkeep, own)):
        rows = block_at(side, quarter)
        arrived = recv_ref[rows, 2 * model : 3 * model].astype(F32)
        target.ref[:, :model] = (matmul(n1t_ref[rows, :], gv_ref[...]) + arrived).astype(BF16)
        arrived = recv_ref[rows, 3 * model : 4 * model].astype(F32)
        target.ref[:, model : 2 * model] = (matmul(ct_ref[rows, :], att_ref[...]) + arrived).astype(BF16)
        arrived = recv_ref[rows, 4 * model :].astype(F32)
        mine = dproj_ref[block_at(2 * bit_of_wide(0) + side, quarter), :].astype(F32)
        target.ref[:, 2 * model :] = (mine + arrived).astype(BF16)
        target.send()


def start_back_kernel(gain_ref, gq, wq, gk, wk, gv, wv, x, gmid, tok, dgain):
    tok.ref[...] = matmul(gq.ready()[...], wq.ready()[...], NT)
    tok.ref[...] += matmul(gk.ready()[...], wk.ready()[...], NT)
    tok.ref[...] += matmul(gv.ready()[...], wv.ready()[...], NT)
    dgain.ref[...] = jnp.zeros_like(dgain.ref)
    x_ref, gmid_ref, gain = x.ready(), gmid.ready(), line_of(gain_ref)
    quarter = x_ref.shape[0] // 4

    def norm(rows):
        grad, shares = norm_back(x_ref[rows, :].astype(F32), gain, tok.ref[rows, :])
        tok.ref[rows, :] = gmid_ref[rows, :] + grad
        dgain.ref[...] += shares

    for i in range(2):
        norm(slice(2 * i * quarter, 2 * (i + 1) * quarter))
        tok.send((pl.ds(2 * i * quarter, 2 * quarter),))


def bias_grad_of(folded, buckets, length):
    heads = folded.shape[0]
    place = jnp.arange(2 * length, dtype=jnp.int32)[None, :] - jnp.arange(8, dtype=jnp.int32)[:, None]
    place = (place + 128) % (2 * length)
    onehot = bucket_of(length - place)[:, :, None] == jnp.arange(buckets, dtype=jnp.int32)
    return jnp.dot(
        folded.reshape(heads, -1), onehot.reshape(-1, buckets).astype(F32), precision=HIGHEST
    ).T


def match(query_emb, picked, mask, positive):
    inverse = 1.0 / math.sqrt(query_emb.shape[-1])
    scores = jnp.einsum("aip,bakp->abki", query_emb, picked, preferred_element_type=F32) * inverse
    best = jax.nn.logsumexp(scores, axis=2)
    values = mask.astype(F32)
    weight = values / jnp.maximum(jnp.sum(values, axis=-1, keepdims=True), 1.0)
    logits = jnp.sum(best * weight[:, None, :], axis=-1) / SOFTMAX_TEMP
    partition = jax.nn.logsumexp(logits, axis=1)
    target = (
        jnp.arange(logits.shape[1], dtype=jnp.int32)[None, :] == positive[:, None]
    ).astype(F32)
    losses = partition - jnp.sum(logits * target, axis=1)
    grad_scores = (jnp.exp(logits - partition[:, None]) - target) / SOFTMAX_TEMP
    soft = jnp.exp(scores - best[:, :, None, :])
    grad_tokens = (grad_scores[:, :, None, None] * weight[:, None, None, :] * soft).astype(BF16)
    own = jnp.einsum("abki,bakp->aip", grad_tokens, picked, preferred_element_type=F32) * inverse
    picks = jnp.einsum("abki,aip->bakp", grad_tokens, query_emb, preferred_element_type=F32) * inverse
    return losses, own.astype(BF16), picks.astype(BF16)


def per_device(
    tokens,
    doc_segments,
    query_mask,
    positives,
    top_index,
    query_weight,
    key_weight,
    value_weight,
    output_weight,
    gate_weight,
    up_weight,
    down_weight,
    projection,
    attention_gain,
    feedforward_gain,
    final_gain,
    bias_table,
):
    length, model = tokens.shape[2], tokens.shape[3]
    heads = bias_table.shape[1]
    query_len = query_mask.shape[1]
    embed = projection.shape[1]
    hidden_width = gate_weight.shape[1]
    top = top_index.shape[2]
    width = lax.axis_size("wide")
    bits = width.bit_length() - 1
    row_queries = length // query_len
    half = row_queries // 2
    stream = lax.axis_index("stream")
    place = lax.axis_index("wide")
    is_query = stream == 0
    gain1, gain2, gain3 = (Small(g.reshape(-1, 128)) for g in (attention_gain, feedforward_gain, final_gain))
    part = 512
    order = tuple(range(bits))
    down_order = (0, 2, 1) + order[3:]

    inputs = tokens.reshape(length, model)
    flat = shape_of(length, model)
    flat32 = shape_of(length, model, dtype=F32)
    wide_flat = shape_of(length, hidden_width)
    shares = shape_of(8, model, dtype=F32)
    square = pltpu.VMEM((length, length), F32)
    pair_sems = pltpu.SemaphoreType.DMA((heads // 2,))
    all_probs = pltpu.VMEM((heads, length, length), BF16)
    picks = top_index.reshape(width, 2, half, top).transpose(1, 0, 2, 3).reshape(-1, 128)
    (
        normed_one, queries, keys, values, context, probs, middle, normed_two, up_factor, gate_factor, hidden, block_out,
        normed_three, lower, upper, picked,
    ) = call(
        partial(forward_kernel, query_len, part),
        [flat] * 5 + [shape_of(heads, length, length), flat32, flat, wide_flat, wide_flat, wide_flat, flat32, flat,
         shape_of(length // 2, embed), shape_of(length // 2, embed), shape_of(picks.size, embed)],
        scratch=[
            square, pltpu.VMEM((heads, 1, 2 * length), F32), pltpu.VMEM((2, 128, 2 * length), F32),
            pltpu.VMEM((2, length, length), F32), all_probs,
            pair_sems, pltpu.VMEM((length, part), F32), pltpu.VMEM((length, part), F32), pltpu.VMEM((length, embed), BF16),
        ],
        name="forward", us=25, raw_results=(5,),
    )(
        bias_table.T, Small(doc_segments), gain1, gain2, gain3, Small(picks), inputs, query_weight, key_weight,
        value_weight, output_weight, gate_weight, up_weight, down_weight, projection,
    )

    other_half = flip_stream(upper)
    both = ("stream", "wide")
    gathered = lax.all_to_all(picked.reshape(2 * width, half * top, embed), both, 0, 0, tiled=True)
    query_emb = jnp.where(is_query, lower, other_half)
    start = place * row_queries + stream * half
    losses, own_grads, pick_grads = match(
        query_emb.reshape(half, query_len, embed),
        gathered[width:].reshape(width, half, top, embed),
        lax.dynamic_slice_in_dim(query_mask, start, half, 0),
        lax.dynamic_slice_in_dim(positives, start, half, 0),
    )
    pick_grads = pick_grads.reshape(width, half * top, embed)
    returned = lax.all_to_all(
        jnp.concatenate([jnp.zeros_like(pick_grads), pick_grads], axis=0), both, 0, 0, tiled=True
    )
    loss_high = losses.astype(BF16)
    loss_low = (losses - loss_high.astype(F32)).astype(BF16)
    other_loss = flip_stream(jnp.stack([loss_high, loss_low])).astype(F32)
    other_loss = other_loss[0] + other_loss[1]
    query_loss = jnp.where(
        is_query,
        jnp.concatenate([losses, other_loss]),
        jnp.concatenate([other_loss, losses]),
    )
    own_grads = own_grads.reshape(length // 2, embed)
    other_grads = flip_stream(own_grads)

    source = blocks_ordered(jnp.arange(model, dtype=jnp.int32), width, order).reshape(1, model)
    tall = shape_of(model, length)
    n1_t, n2_t, n3_t, context_t, onehot = call(
        turn_kernel, [tall] * 4 + [shape_of(length, picks.size)], scratch=[pltpu.VMEM((model, model), BF16)], name="turn", us=4
    )(Small(source), Small(picks), normed_one, normed_two, normed_three, context)
    hidden_t = blocks_ordered(hidden.T, width, down_order)

    def core():
        return bit_of_wide(0)

    def other_core():
        return 1 - bit_of_wide(0)

    many = picks.size > 2048
    onehot_operand = Raw(onehot) if many else onehot
    pieces_of_picks = [pltpu.VMEM((length, 2048), BF16), pltpu.SemaphoreType.DMA] if many else []
    half_rows = shape_of(model // 2, hidden_width)
    (
        down_send, branch, grad_gate, grad_up, gate_send, up_send, grad_projection, grad_middle, attended,
        grad_context, shares2, shares3,
    ) = call(
        partial(upper_back_kernel, part),
        [shape_of(hidden_width // 2, model), flat, wide_flat, wide_flat, half_rows,
         half_rows, shape_of(model, embed), flat32, flat, flat, shares,
         shares],
        scratch=[
            pltpu.VMEM((length, embed), BF16), pltpu.VMEM((length, model), F32), pltpu.VMEM((length, part), F32),
            pltpu.VMEM((length, embed), F32),
        ]
        + pieces_of_picks,
        name="upper_back", us=18, after=(other_loss,), pieces={9: (0, 4), 10: (1, 4), 11: (1, 4)},
    )(
        Small(projection), gain2, gain3, own_grads, other_grads, returned.reshape(-1, embed), onehot_operand, block_out,
        Part(hidden_t, other_core, hidden_width // 2), down_weight, up_factor, gate_factor,
        Part(n2_t, other_core, model // 2), n3_t, gate_weight, up_weight, middle, output_weight,
    )
    down_recv = flip_wide(down_send, 0)
    gate_recv = flip_wide(gate_send, 0)
    up_recv = flip_wide(up_send, 0)

    down_send, down_keep = call(
        down_keep_kernel, [shape_of(hidden_width // 4, model)] * 2, name="down_keep", us=4
    )(branch, Part(hidden_t, core, hidden_width // 2), down_recv)
    down_recv = flip_wide(down_send, 2)

    gate_send, gate_keep, up_send, up_keep = call(
        partial(gates_keep_kernel, part),
        [shape_of(model // 2, hidden_width // 2)] * 2 + [shape_of(model // 4, hidden_width)] * 2,
        name="gates_keep", us=6, after=(down_keep,),
    )(Part(n2_t, core, model // 2), grad_gate, gate_recv, grad_up, up_recv)
    gate_recv = flip_stream(gate_send)
    up_recv = flip_wide(up_send, 1)

    widest = 4 * model + embed
    grad_queries, grad_keys, grad_values, folded, heads_send = call(
        attend_back_kernel,
        [flat, flat, flat, shape_of(heads, 8, 2 * length, dtype=F32), shape_of(model // 2, widest)],
        scratch=[
            all_probs, pair_sems, pltpu.VMEM((2, length, length), BF16), pltpu.VMEM((2, length, length), F32),
            pltpu.VMEM((2, 128, 2 * length), F32),
        ],
        name="attend_back", us=14, after=(up_keep,),
    )(
        Small(grad_projection), Raw(probs), queries, keys, values, grad_context, Part(n1_t, other_core, model // 2),
        Part(context_t, other_core, model // 2), attended,
    )
    down_sum = halve_rows(added(down_keep, down_recv), 1)
    heads_recv = flip_wide(heads_send, 0)
    gate_sum = added(gate_keep, gate_recv)
    up_sum = added(up_keep, up_recv)
    grad_tokens, shares1 = call(
        start_back_kernel, [flat32, shares], name="start_back", us=5, after=(heads_send, down_sum, gate_recv, up_recv)
    )(gain1, grad_queries, query_weight, grad_keys, key_weight, grad_values, value_weight, inputs, grad_middle)
    a_send, a_keep, b_send, b_keep, gain_grads = call(
        heads_keep_kernel,
        [shape_of(model // 2, model)] * 2 + [shape_of(model // 4, 2 * model + embed)] * 2
        + [shape_of(3, model, dtype=F32)],
        name="heads_keep", us=4, after=(grad_tokens,),
    )(
        Small(grad_projection), Small(shares1), Small(shares2), Small(shares3), Part(n1_t, core, model // 2),
        Part(context_t, core, model // 2), grad_queries, grad_keys, grad_values, attended, heads_recv,
    )
    a_sum = added(a_keep, flip_stream(a_send))
    b_sum = added(b_keep, flip_wide(b_send, 1))

    for bit in down_order[3:]:
        down_sum = halve_rows(down_sum, bit)
    down_sum = down_sum.astype(F32) + flip_stream(down_sum).astype(F32)

    def finish(first, second):
        block = jnp.concatenate([halve_rows(first, 1), second], axis=1)
        for bit in range(2, bits):
            block = halve_rows(block, bit)
        other = flip_stream(block)
        edge = first.shape[1]
        mine, theirs = block[:, :edge].astype(F32), other[:, :edge].astype(F32)
        left, right = jnp.where(is_query, mine, theirs), jnp.where(is_query, theirs, mine)
        return left, right, block[:, edge:].astype(F32) + other[:, edge:].astype(F32)

    gate_left, gate_right, sum_up = finish(gate_sum, up_sum)
    sum_query, sum_key, rest = finish(a_sum, b_sum)
    grad_table = bias_grad_of(folded, bias_table.shape[0], length)
    small = jnp.concatenate([gain_grads.reshape(-1), grad_table.reshape(-1)])
    small = sum_everywhere(small.reshape(-1, 128), width).reshape(-1)
    own_rows = model // width
    grad_gains = [lax.dynamic_slice_in_dim(small, i * model + place * own_rows, own_rows, 0) for i in range(3)]
    return (
        query_loss,
        grad_tokens.reshape(tokens.shape),
        sum_query,
        sum_key,
        rest[:, :model],
        rest[:, model : 2 * model],
        jnp.concatenate([gate_left, gate_right], axis=1),
        sum_up,
        down_sum,
        rest[:, 2 * model :],
        grad_gains[0],
        grad_gains[1],
        grad_gains[2],
        small[3 * model :].reshape(bias_table.shape),
    )


def solution(mesh):
    rows = P("wide", None)
    in_specs = (
        P("stream", "wide", None, None),
        rows,
        P(),
        P(),
        P(None, "wide", None),
    ) + (P(),) * 12
    out_specs = (P("wide"), P("stream", "wide", None, None)) + (rows,) * 8 + (P("wide"),) * 3 + (P(),)
    return jax.shard_map(
        per_device, mesh=mesh, in_specs=in_specs, out_specs=out_specs, check_vma=False
    )
```

```python
from functools import partial
import math

import jax
import jax.numpy as jnp
import numpy as np
from jax import lax
from jax.experimental import pallas as pl
from jax.experimental.pallas import tpu as pltpu
from jax.sharding import PartitionSpec as P

EPSILON = 1e-06
SOFTMAX_TEMP = 0.05
MASKED_SCORE = -1e30
HIGHEST = lax.Precision.HIGHEST
BF16 = jnp.bfloat16
F32 = jnp.float32
NT = (((1,), (1,)), ((), ()))
TN = (((0,), (0,)), ((), ()))


def matmul(left, right, dims=(((1,), (0,)), ((), ()))):
    return lax.dot_general(left, right, dims, preferred_element_type=F32)


def flip_stream(block):
    return lax.ppermute(block, "stream", [(0, 1), (1, 0)])


def flip_wide(block, bit):
    devices = range(lax.axis_size("wide"))
    return lax.ppermute(block, "wide", [(i, i ^ (1 << bit)) for i in devices])


def added(kept, received):
    return (kept.astype(F32) + received.astype(F32)).astype(BF16)


def blocks_ordered(rows, width, order):
    bits = width.bit_length() - 1
    shaped = rows.reshape((2,) * bits + (rows.shape[0] // width,) + rows.shape[1:])
    axes = tuple(bits - 1 - bit for bit in order) + tuple(range(bits, shaped.ndim))
    return shaped.transpose(axes).reshape(rows.shape)


def halve_rows(block, bit):
    own = (lax.axis_index("wide") >> bit) & 1
    half = block.shape[0] // 2
    sent = lax.dynamic_slice_in_dim(block, (1 - own) * half, half, 0)
    kept = lax.dynamic_slice_in_dim(block, own * half, half, 0)
    return added(kept, flip_wide(sent, bit))


def sum_everywhere(block, width):
    block = block + flip_stream(block)
    for bit in range(width.bit_length() - 1):
        block = block + flip_wide(block, bit)
    return block


class Small:
    def __init__(self, array):
        self.array = array


class Raw:
    def __init__(self, array):
        self.array = array


class Arrived:
    def __init__(self, array):
        self.array = array


class Part:
    def __init__(self, array, number, size):
        self.array, self.number, self.size = array, number, size


class Fetched:
    def __init__(self, source, target, semaphores, axis, pieces):
        size = target.shape[axis] // pieces
        at = [(slice(None),) * axis + (pl.ds(i * size, size),) for i in range(pieces)]
        self.target = target
        self.copies = [
            pltpu.make_async_copy(source.at[at[i]], target.at[at[i]], semaphores[i]) for i in range(pieces)
        ]
        for copy in self.copies:
            copy.start()

    def piece(self, i):
        if self.copies[i] is not None:
            self.copies[i].wait()
            self.copies[i] = None
        return self.target

    def ready(self):
        for i in range(len(self.copies)):
            self.piece(i)
        return self.target


class Result:
    def __init__(self, ref, target, semaphores):
        self.ref, self.target, self.semaphores = ref, target, semaphores
        self.copies = []

    def send(self, at=(slice(None),)):
        copy = pltpu.make_async_copy(self.ref.at[at], self.target.at[at], self.semaphores[len(self.copies)])
        copy.start()
        self.copies.append(copy)


def call(kernel, out_shape, scratch=(), name=None, after=(), us=5, pieces=None, raw_results=(), limit=56):
    pieces = pieces or {}

    def built(*operands):
        taken, results = len(operands), len(out_shape)
        arrays, buffers, semaphores = [], [], 0
        for i, operand in enumerate(operands):
            wrapped = isinstance(operand, Small | Raw | Part | Arrived)
            array = operand.array if wrapped else operand
            arrays.append(array if isinstance(operand, Small | Arrived) else pltpu.with_memory_space_constraint(array, pltpu.HBM))
            if not isinstance(operand, Small | Raw):
                rows = operand.size if isinstance(operand, Part) else array.shape[0]
                buffers.append(pltpu.VMEM((rows,) + array.shape[1:], array.dtype))
                semaphores += pieces.get(i, (0, 1))[1]
        fetched = len(buffers)
        send_at = semaphores
        for i, out in enumerate(out_shape):
            if i not in raw_results:
                buffers.append(pltpu.VMEM(out.shape, out.dtype))
                semaphores += 4

        def run(*refs):
            outputs = refs[taken + len(after) : taken + len(after) + results]
            rest = refs[taken + len(after) + results :]
            slots, sems, own = rest[: len(buffers)], rest[len(buffers)], rest[len(buffers) + 1 :]
            given, place, at = [], 0, 0
            for i, operand in enumerate(operands):
                if isinstance(operand, Small | Raw):
                    given.append(refs[i])
                    continue
                source = refs[i]
                if isinstance(operand, Part):
                    source = source.at[block_at(operand.number(), operand.size)]
                axis, count = pieces.get(i, (0, 1))
                given.append(Fetched(source, slots[place], [sems.at[at + j] for j in range(count)], axis, count))
                place, at = place + 1, at + count
            made, at = [], send_at
            for i, output in enumerate(outputs):
                if i in raw_results:
                    made.append(output)
                    continue
                made.append(Result(slots[place], output, [sems.at[at + j] for j in range(4)]))
                place, at = place + 1, at + 4
            kernel(*given, *made, *own)
            for operand in given:
                if isinstance(operand, Fetched):
                    operand.ready()
            for i, result in enumerate(made):
                if i not in raw_results:
                    if not result.copies:
                        result.send()
                    for copy in result.copies:
                        copy.wait()

        return pl.pallas_call(
            run,
            in_specs=[pl.BlockSpec(memory_space=pltpu.VMEM if isinstance(x, Small) else pl.ANY) for x in operands]
            + [pl.BlockSpec(memory_space=pl.ANY)] * len(after),
            out_specs=[pl.BlockSpec(memory_space=pl.ANY)] * results,
            out_shape=[pltpu.HBM(x.shape, x.dtype) for x in out_shape],
            scratch_shapes=buffers + [pltpu.SemaphoreType.DMA((max(semaphores, 1),))] + list(scratch),
            compiler_params=pltpu.CompilerParams(vmem_limit_bytes=limit << 20),
            cost_estimate=pl.CostEstimate(flops=0, bytes_accessed=int(us * 3.3e6), transcendentals=0),
            name=name,
        )(*arrays, *after)

    return built


def shape_of(*shape, dtype=BF16):
    return jax.ShapeDtypeStruct(shape, dtype)


def tiles(total, size, body):
    def step(i, carry):
        body(pl.ds(pl.multiple_of(i * size, size), size))
        return carry

    lax.fori_loop(0, total // size, step, 0, unroll=2)


def block_at(index, size):
    return pl.ds(pl.multiple_of(index * size, size), size)


def bit_of_wide(bit):
    return (lax.axis_index("wide") >> bit) & 1


def normed(values, gain):
    inverse = lax.rsqrt(jnp.mean(values * values, axis=-1, keepdims=True) + EPSILON)
    return values * inverse * gain


def norm_back(values, gain, upstream):
    inverse = lax.rsqrt(jnp.mean(values * values, axis=-1, keepdims=True) + EPSILON)
    unit = values * inverse
    weighted = upstream * gain
    inner = jnp.mean(weighted * unit, axis=-1, keepdims=True)
    shares = (upstream * unit).reshape(-1, 8, values.shape[1]).sum(axis=0)
    return (weighted - unit * inner) * inverse, shares


def bucket_of(offset):
    distance = jnp.abs(offset)
    far_bucket = jnp.full(offset.shape, 8, jnp.int32)
    for exponent in range(1, 8):
        far_bucket = far_bucket + (distance * distance >= 64 * 2**exponent).astype(jnp.int32)
    near_bucket = jnp.where(distance < 8, distance, far_bucket)
    return near_bucket + 16 * (offset > 0).astype(jnp.int32)


def line_of(gain_ref):
    return jnp.concatenate([gain_ref[i : i + 1, :] for i in range(gain_ref.shape[0])], axis=1)


def forward_kernel(query_len, part, table, seg_ref, gain1_ref, gain2_ref, gain3_ref, picks_ref, x, wq, wk, wv, wo, wg, wu,
                   wd, proj, n1, q, k, v, ctx, probs_out, mid, n2, up_factor, gate_factor, hidden, out, n3, lower, upper, picked,
                   mask_ref, line_ref, base_ref, score_ref, probs_ref, probs_sem, gate_ref, up_ref, emb_ref):
    x_ref = x.ready()
    length, model = x_ref.shape
    blocks = length // 128
    table_ref = table.target
    heads = table_ref.shape[0]
    gain = line_of(gain1_ref)

    def norm(rows):
        n1.ref[rows, :] = normed(x_ref[rows, :].astype(F32), gain).astype(BF16)

    tiles(length, 256, norm)
    n1.send()
    for result, weight in ((q, wq), (k, wk), (v, wv)):
        result.ref[...] = matmul(n1.ref[...], weight.ready()[...]).astype(BF16)
        result.send()

    lane = lax.broadcasted_iota(jnp.int32, (1, length), 1)
    segments = jnp.where(lax.axis_index("stream") == 0, lane // query_len, seg_ref[...])
    for a in range(blocks):
        column = jnp.broadcast_to(segments[:, 128 * a : 128 * a + 128], (128, 128)).T[:, 0:1]
        mask_ref[128 * a : 128 * a + 128, :] = jnp.where(column == segments, 0.0, MASKED_SCORE)
    offsets = length - lax.broadcasted_iota(jnp.int32, (1, 2 * length), 1)
    buckets = lax.broadcasted_iota(jnp.int32, (table_ref.shape[1], 2 * length), 0)
    onehot = jnp.where(bucket_of(offsets) == buckets, 1.0, 0.0)
    lines = jnp.dot(table.ready()[...], onehot, precision=HIGHEST, preferred_element_type=F32)
    for head in range(heads):
        line_ref[head] = lines[head : head + 1, :]
    first = lax.broadcasted_iota(jnp.int32, (1, 128), 1) < 64

    def probs_copy(p):
        at = pl.ds(2 * p, 2)
        return pltpu.make_async_copy(probs_ref.at[at], probs_out.at[at], probs_sem.at[p])

    def pair(p, carry):
        own_lanes = block_at(p, 128)
        queries, keys, values = q.ref[:, own_lanes], k.ref[:, own_lanes], v.ref[:, own_lanes]
        contexts = []
        for head in range(2):
            line = jnp.broadcast_to(line_ref[2 * p + head], (128, 2 * length))
            base_ref[head] = pltpu.roll(line, 2 * length - 128, 1, stride=1, stride_axis=0)
            own = jnp.where(first == (head == 0), queries, jnp.zeros_like(queries))
            score_ref[head] = matmul(keys, own, NT)
            for t in range(blocks):
                lanes = slice(128 * t, 128 * t + 128)
                scores = []
                for a in range(blocks):
                    rows = slice(128 * a, 128 * a + 128)
                    start = length - 128 - 128 * a + 128 * t
                    scores.append(score_ref[head, rows, lanes] + base_ref[head, :, start : start + 128] + mask_ref[rows, lanes])
                top = scores[0].max(axis=0, keepdims=True)
                for block in scores[1:]:
                    top = jnp.maximum(top, block.max(axis=0, keepdims=True))
                total = jnp.zeros_like(top)
                for a in range(blocks):
                    scores[a] = jnp.exp(scores[a] - top)
                    total = total + scores[a].sum(axis=0, keepdims=True)
                inverse = 1.0 / total
                for a in range(blocks):
                    probs_ref[2 * p + head, 128 * a : 128 * a + 128, lanes] = (scores[a] * inverse).astype(BF16)
            contexts.append(matmul(probs_ref[2 * p + head], values, TN))
        ctx.ref[:, own_lanes] = jnp.where(first, contexts[0], contexts[1]).astype(BF16)
        probs_copy(p).start()
        return carry

    lax.fori_loop(0, heads // 2, pair, 0, unroll=3)
    ctx.send()
    mid.ref[...] = matmul(ctx.ref[...], wo.ready()[...])
    gain = line_of(gain2_ref)

    def start(rows):
        middle = x_ref[rows, :].astype(F32) + mid.ref[rows, :]
        mid.ref[rows, :] = middle
        n2.ref[rows, :] = normed(middle, gain).astype(BF16)

    tiles(length, 256, start)
    mid.send()
    n2.send()
    scale = math.sqrt(2.0 / math.pi)
    wg_ref, wu_ref = wg.ready(), wu.ready()

    def column(columns):
        gate_ref[...] = matmul(n2.ref[...], wg_ref[:, columns])
        up_ref[...] = matmul(n2.ref[...], wu_ref[:, columns])

        def gelu(rows):
            u, up = gate_ref[rows, :], up_ref[rows, :]
            squared = u * u
            tanh = jnp.tanh(scale * u * (1.0 + 0.044715 * squared))
            gate = 0.5 * (1.0 + tanh)
            slope = gate + 0.5 * u * (1.0 - tanh * tanh) * (scale * (1.0 + 3 * 0.044715 * squared))
            value = u * gate
            up_factor.ref[rows, columns] = value.astype(BF16)
            gate_factor.ref[rows, columns] = (up * slope).astype(BF16)
            hidden.ref[rows, columns] = (value * up).astype(BF16)

        tiles(length, 32, gelu)

    tiles(wg_ref.shape[1], part, column)
    for result in (hidden, up_factor, gate_factor):
        result.send()
    out.ref[...] = matmul(hidden.ref[...], wd.ready()[...])
    gain = line_of(gain3_ref)

    def end(rows):
        value = out.ref[rows, :] + mid.ref[rows, :]
        out.ref[rows, :] = value
        n3.ref[rows, :] = normed(value, gain).astype(BF16)

    tiles(length, 256, end)
    out.send()
    n3.send()
    emb_ref[...] = matmul(n3.ref[...], proj.ready()[...]).astype(BF16)
    lower.ref[...] = emb_ref[: length // 2, :]
    upper.ref[...] = emb_ref[length // 2 :, :]
    lower.send()
    upper.send()
    tokens = lax.broadcasted_iota(jnp.int32, (1, 128), 1)

    def pick(i, carry):
        column = jnp.broadcast_to(picks_ref[pl.ds(i, 1), :], (128, 128)).T
        onehot = jnp.concatenate(
            [jnp.where(column == tokens + 128 * t, 1.0, 0.0).astype(BF16) for t in range(blocks)], axis=1
        )
        picked.ref[block_at(i, 128), :] = matmul(onehot, emb_ref[...]).astype(BF16)
        return carry

    lax.fori_loop(0, picks_ref.shape[0], pick, 0, unroll=8 if picks_ref.shape[0] % 8 == 0 else 1)
    picked.send()
    for p in range(heads // 2):
        probs_copy(p).wait()


def turn_kernel(source_ref, picks_ref, *refs):
    onehot, refs = refs[-2], refs[:-2] + refs[-1:]
    count = (len(refs) - 1) // 2
    tokens = lax.broadcasted_iota(jnp.int32, (onehot.ref.shape[0], 128), 0)

    def pick(i, carry):
        onehot.ref[:, block_at(i, 128)] = jnp.where(picks_ref[pl.ds(i, 1), :] == tokens, 1.0, 0.0).astype(BF16)
        return carry

    lax.fori_loop(0, picks_ref.shape[0], pick, 0)
    onehot.send()
    order_ref = refs[-1]
    size = source_ref.shape[1]
    for i in range(size // 128):
        column = jnp.broadcast_to(source_ref[:, 128 * i : 128 * i + 128], (128, 128)).T
        for j in range(size // 128):
            lane = lax.broadcasted_iota(jnp.int32, (1, 128), 1) + 128 * j
            order_ref[128 * i : 128 * i + 128, 128 * j : 128 * j + 128] = jnp.where(column == lane, 1.0, 0.0).astype(BF16)
    for taken, made in zip(refs[:count], refs[count : 2 * count]):
        made.ref[...] = matmul(order_ref[...], taken.ready()[...], NT).astype(BF16)
        made.send()


def upper_back_kernel(part, proj_ref, gain2_ref, gain3_ref, own, other, returned, onehot, block, ht, wd, upf, gatef,
                      n2t, n3t, wg, wu, mid, wo, dsent, branch, gg, gu, sg, su, dproj, gmid, att, gctx, dgain2, dgain3,
                      emb_ref, gout_ref, grad_ref, doc_ref, piece_ref=None, piece_sem=None):
    length = gmid.ref.shape[0]
    half = length // 2
    is_query = lax.axis_index("stream") == 0
    returned_ref = returned.ready()
    if isinstance(onehot, Fetched):
        doc_ref[...] = matmul(onehot.ready()[...], returned_ref[...])
    else:
        size = piece_ref.shape[1]
        doc_ref[...] = jnp.zeros_like(doc_ref)

        def add(i, carry):
            copy = pltpu.make_async_copy(onehot.at[:, block_at(i, size)], piece_ref, piece_sem)
            copy.start()
            copy.wait()
            doc_ref[...] += matmul(piece_ref[...], returned_ref[block_at(i, size), :])
            return carry

        lax.fori_loop(0, returned_ref.shape[0] // size, add, 0)
    for side, query in enumerate((own, other)):
        rows = slice(side * half, side * half + half)
        emb_ref[rows, :] = jnp.where(is_query, query.ready()[...], doc_ref[rows, :].astype(BF16))
    gout_ref[...] = matmul(emb_ref[...], proj_ref[...], NT)
    dgain2.ref[...] = jnp.zeros_like(dgain2.ref)
    dgain3.ref[...] = jnp.zeros_like(dgain3.ref)
    block_ref, gain3 = block.ready(), line_of(gain3_ref)

    def norm3(rows):
        grad, shares = norm_back(block_ref[rows, :], gain3, gout_ref[rows, :])
        dgain3.ref[...] += shares
        gout_ref[rows, :] = grad
        branch.ref[rows, :] = grad.astype(BF16)

    tiles(length, 256, norm3)
    branch.send()
    dsent.ref[...] = matmul(ht.ready()[...], branch.ref[...]).astype(BF16)
    dsent.send()

    for i in range(gg.ref.shape[1] // part):
        columns = slice(i * part, i * part + part)
        grad_ref[...] = matmul(branch.ref[...], wd.piece(i)[columns, :], NT)
        upf_ref, gatef_ref = upf.piece(i), gatef.piece(i)

        def factors(rows):
            grad = grad_ref[rows, :]
            gu.ref[rows, columns] = (grad * upf_ref[rows, columns].astype(F32)).astype(BF16)
            gg.ref[rows, columns] = (grad * gatef_ref[rows, columns].astype(F32)).astype(BF16)

        tiles(length, 64, factors)
    n2t_ref = n2t.ready()
    sg.ref[...] = matmul(n2t_ref[...], gg.ref[...]).astype(BF16)
    su.ref[...] = matmul(n2t_ref[...], gu.ref[...]).astype(BF16)
    gg.send()
    gu.send()
    sg.send()
    dproj.ref[...] = matmul(n3t.ready()[...], emb_ref[...]).astype(BF16)
    dproj.send()
    su.send()

    gmid.ref[...] = matmul(gg.ref[...], wg.ready()[...], NT)
    gmid.ref[...] += matmul(gu.ref[...], wu.ready()[...], NT)
    mid_ref, gain2 = mid.ready(), line_of(gain2_ref)

    def norm2(rows):
        grad, shares = norm_back(mid_ref[rows, :], gain2, gmid.ref[rows, :])
        grad = grad + gout_ref[rows, :]
        dgain2.ref[...] += shares
        gmid.ref[rows, :] = grad
        att.ref[rows, :] = grad.astype(BF16)

    tiles(length, 256, norm2)
    gmid.send()
    att.send()
    gctx.ref[...] = matmul(att.ref[...], wo.ready()[...], NT).astype(BF16)


def down_keep_kernel(branch, ht, recv, sent, keep):
    half = sent.ref.shape[0]
    own = bit_of_wide(2)
    branch_ref, ht_ref, recv_ref = branch.ready(), ht.ready(), recv.ready()
    for target, side in ((sent, 1 - own), (keep, own)):
        rows = block_at(side, half)
        target.ref[...] = (matmul(ht_ref[rows, :], branch_ref[...]) + recv_ref[rows, :].astype(F32)).astype(BF16)
        target.send()


def gates_keep_kernel(part, n2t, gg, rg, gu, ru, gs, gk, us, uk):
    columns = gs.ref.shape[1]
    quarter = us.ref.shape[0]
    own, stream = bit_of_wide(1), lax.axis_index("stream")
    n2t_ref, gg_ref, rg_ref = n2t.ready(), gg.ready(), rg.ready()
    for target, side in ((gs, 1 - stream), (gk, stream)):
        for i in range(columns // part):
            local = slice(i * part, i * part + part)
            there = block_at(side * (columns // part) + i, part)
            made = matmul(n2t_ref[...], gg_ref[:, there])
            target.ref[:, local] = (made + rg_ref[:, there].astype(F32)).astype(BF16)
        target.send()
    gu_ref, ru_ref = gu.ready(), ru.ready()
    for target, side in ((us, 1 - own), (uk, own)):
        rows = block_at(side, quarter)
        for i in range(gu_ref.shape[1] // part):
            local = slice(i * part, i * part + part)
            made = matmul(n2t_ref[rows, :], gu_ref[:, local])
            target.ref[:, local] = (made + ru_ref[rows, local].astype(F32)).astype(BF16)
        target.send()


def attend_back_kernel(dproj_ref, probs_in, q, k, v, g, n1t, ct, att, gq, gk, gv, bias, sent,
                       probs_ref, probs_sem, gs_ref, gp_ref, acc_ref):
    def probs_copy(p):
        at = pl.ds(2 * p, 2)
        return pltpu.make_async_copy(probs_in.at[at], probs_ref.at[at], probs_sem.at[p])

    pairs = probs_ref.shape[0] // 2
    for p in range(pairs):
        probs_copy(p).start()
    q_ref, k_ref, v_ref, g_ref = q.ready(), k.ready(), v.ready(), g.ready()
    length = q_ref.shape[0]
    blocks = length // 128
    first = lax.broadcasted_iota(jnp.int32, (1, 128), 1) < 64
    acc_ref[:, :, (2 * blocks - 1) * 128 :] = jnp.zeros((2, 128, 128), F32)

    def pair(p, carry):
        own_lanes = block_at(p, 128)
        queries, keys = q_ref[:, own_lanes], k_ref[:, own_lanes]
        values, grads = v_ref[:, own_lanes], g_ref[:, own_lanes]
        grad_queries, grad_keys, grad_values = [], [], []
        probs_copy(p).wait()
        for head in range(2):
            own = jnp.where(first == (head == 0), grads, jnp.zeros_like(grads))
            gp_ref[head] = matmul(values, own, NT)
            for t in range(blocks):
                lanes = slice(128 * t, 128 * t + 128)
                inner = jnp.zeros((1, 128), F32)
                products = []
                for a in range(blocks):
                    rows = slice(128 * a, 128 * a + 128)
                    product = gp_ref[head, rows, lanes] * probs_ref[2 * p + head, rows, lanes].astype(F32)
                    inner = inner + product.sum(axis=0, keepdims=True)
                    products.append(product)
                for a in range(blocks):
                    rows = slice(128 * a, 128 * a + 128)
                    grad_scores = products[a] - probs_ref[2 * p + head, rows, lanes].astype(F32) * inner
                    gs_ref[head, rows, lanes] = grad_scores.astype(BF16)
                    start = length - 128 - 128 * a + 128 * t
                    if t == 0 or a == 0:
                        acc_ref[head, :, start : start + 128] = grad_scores
                    else:
                        acc_ref[head, :, start : start + 128] += grad_scores
            grad_values.append(matmul(probs_ref[2 * p + head], grads))
            grad_keys.append(matmul(gs_ref[head], queries))
            grad_queries.append(matmul(gs_ref[head], keys, TN))
            folded = acc_ref[head, 0:8, :]
            for c in range(1, 16):
                folded = folded + pltpu.roll(acc_ref[head, 8 * c : 8 * c + 8, :], 2 * length - 8 * c, 1)
            bias.ref[2 * p + head] = folded
        gq.ref[:, own_lanes] = jnp.where(first, grad_queries[0], grad_queries[1]).astype(BF16)
        gk.ref[:, own_lanes] = jnp.where(first, grad_keys[0], grad_keys[1]).astype(BF16)
        gv.ref[:, own_lanes] = jnp.where(first, grad_values[0], grad_values[1]).astype(BF16)
        return carry

    lax.fori_loop(0, pairs, pair, 0)
    for result in (gq, gk, gv, bias):
        result.send()
    half, model = sent.ref.shape[0], q_ref.shape[1]
    n1t_ref, ct_ref, att_ref = n1t.ready(), ct.ready(), att.ready()
    for place, (left, right) in enumerate(((n1t_ref, gq.ref), (n1t_ref, gk.ref), (n1t_ref, gv.ref), (ct_ref, att_ref))):
        sent.ref[:, place * model : (place + 1) * model] = matmul(left[...], right[...]).astype(BF16)
    sent.ref[:, 4 * model :] = dproj_ref[block_at(1 - bit_of_wide(0), half), :]


def heads_keep_kernel(dproj_ref, share1_ref, share2_ref, share3_ref, n1t, ct, gq, gk, gv, att, recv,
                      asent, akeep, bsent, bkeep, dgain):
    for i, share_ref in enumerate((share1_ref, share2_ref, share3_ref)):
        dgain.ref[i : i + 1, :] = jnp.sum(share_ref[...], axis=0, keepdims=True)
    half, model = asent.ref.shape
    quarter = bsent.ref.shape[0]
    own = bit_of_wide(1)
    n1t_ref, gq_ref, gk_ref, recv_ref = n1t.ready(), gq.ready(), gk.ready(), recv.ready()
    grad_query = (matmul(n1t_ref[...], gq_ref[...]) + recv_ref[:, :model].astype(F32)).astype(BF16)
    grad_key = (matmul(n1t_ref[...], gk_ref[...]) + recv_ref[:, model : 2 * model].astype(F32)).astype(BF16)
    first = lax.axis_index("stream") == 0
    asent.ref[...] = jnp.where(first, grad_key, grad_query)
    asent.send()
    akeep.ref[...] = jnp.where(first, grad_query, grad_key)
    akeep.send()
    ct_ref, gv_ref, att_ref = ct.ready(), gv.ready(), att.ready()
    for target, side in ((bsent, 1 - own), (bkeep, own)):
        rows = block_at(side, quarter)
        arrived = recv_ref[rows, 2 * model : 3 * model].astype(F32)
        target.ref[:, :model] = (matmul(n1t_ref[rows, :], gv_ref[...]) + arrived).astype(BF16)
        arrived = recv_ref[rows, 3 * model : 4 * model].astype(F32)
        target.ref[:, model : 2 * model] = (matmul(ct_ref[rows, :], att_ref[...]) + arrived).astype(BF16)
        arrived = recv_ref[rows, 4 * model :].astype(F32)
        mine = dproj_ref[block_at(2 * bit_of_wide(0) + side, quarter), :].astype(F32)
        target.ref[:, 2 * model :] = (mine + arrived).astype(BF16)
        target.send()


def start_back_kernel(gain_ref, gq, wq, gk, wk, gv, wv, x, gmid, tok, dgain):
    tok.ref[...] = matmul(gq.ready()[...], wq.ready()[...], NT)
    tok.ref[...] += matmul(gk.ready()[...], wk.ready()[...], NT)
    tok.ref[...] += matmul(gv.ready()[...], wv.ready()[...], NT)
    dgain.ref[...] = jnp.zeros_like(dgain.ref)
    x_ref, gmid_ref, gain = x.ready(), gmid.ready(), line_of(gain_ref)
    quarter = x_ref.shape[0] // 4

    def norm(rows):
        grad, shares = norm_back(x_ref[rows, :].astype(F32), gain, tok.ref[rows, :])
        tok.ref[rows, :] = gmid_ref[rows, :] + grad
        dgain.ref[...] += shares

    for i in range(2):
        norm(slice(2 * i * quarter, 2 * (i + 1) * quarter))
        tok.send((pl.ds(2 * i * quarter, 2 * quarter),))


def bias_grad_of(folded, buckets, length):
    heads = folded.shape[0]
    place = jnp.arange(2 * length, dtype=jnp.int32)[None, :] - jnp.arange(8, dtype=jnp.int32)[:, None]
    place = (place + 128) % (2 * length)
    onehot = bucket_of(length - place)[:, :, None] == jnp.arange(buckets, dtype=jnp.int32)
    return jnp.dot(
        folded.reshape(heads, -1), onehot.reshape(-1, buckets).astype(F32), precision=HIGHEST
    ).T


def match(query_emb, picked, mask, positive):
    inverse = 1.0 / math.sqrt(query_emb.shape[-1])
    scores = jnp.einsum("aip,bakp->abki", query_emb, picked, preferred_element_type=F32) * inverse
    best = jax.nn.logsumexp(scores, axis=2)
    values = mask.astype(F32)
    weight = values / jnp.maximum(jnp.sum(values, axis=-1, keepdims=True), 1.0)
    logits = jnp.sum(best * weight[:, None, :], axis=-1) / SOFTMAX_TEMP
    partition = jax.nn.logsumexp(logits, axis=1)
    target = (
        jnp.arange(logits.shape[1], dtype=jnp.int32)[None, :] == positive[:, None]
    ).astype(F32)
    losses = partition - jnp.sum(logits * target, axis=1)
    grad_scores = (jnp.exp(logits - partition[:, None]) - target) / SOFTMAX_TEMP
    soft = jnp.exp(scores - best[:, :, None, :])
    grad_tokens = (grad_scores[:, :, None, None] * weight[:, None, None, :] * soft).astype(BF16)
    own = jnp.einsum("abki,bakp->aip", grad_tokens, picked, preferred_element_type=F32) * inverse
    picks = jnp.einsum("abki,aip->bakp", grad_tokens, query_emb, preferred_element_type=F32) * inverse
    return losses, own.astype(BF16), picks.astype(BF16)


def per_device(
    tokens,
    doc_segments,
    query_mask,
    positives,
    top_index,
    query_weight,
    key_weight,
    value_weight,
    output_weight,
    gate_weight,
    up_weight,
    down_weight,
    projection,
    attention_gain,
    feedforward_gain,
    final_gain,
    bias_table,
):
    length, model = tokens.shape[2], tokens.shape[3]
    heads = bias_table.shape[1]
    query_len = query_mask.shape[1]
    embed = projection.shape[1]
    hidden_width = gate_weight.shape[1]
    top = top_index.shape[2]
    width = lax.axis_size("wide")
    bits = width.bit_length() - 1
    row_queries = length // query_len
    half = row_queries // 2
    stream = lax.axis_index("stream")
    place = lax.axis_index("wide")
    is_query = stream == 0
    gain1, gain2, gain3 = (Small(g.reshape(-1, 128)) for g in (attention_gain, feedforward_gain, final_gain))
    part = 512
    order = tuple(range(bits))
    down_order = (0, 2, 1) + order[3:]

    inputs = tokens.reshape(length, model)
    flat = shape_of(length, model)
    flat32 = shape_of(length, model, dtype=F32)
    wide_flat = shape_of(length, hidden_width)
    shares = shape_of(8, model, dtype=F32)
    square = pltpu.VMEM((length, length), F32)
    pair_sems = pltpu.SemaphoreType.DMA((heads // 2,))
    all_probs = pltpu.VMEM((heads, length, length), BF16)
    picks = top_index.reshape(width, 2, half, top).transpose(1, 0, 2, 3).reshape(-1, 128)
    (
        normed_one, queries, keys, values, context, probs, middle, normed_two, up_factor, gate_factor, hidden, block_out,
        normed_three, lower, upper, picked,
    ) = call(
        partial(forward_kernel, query_len, part),
        [flat] * 5 + [shape_of(heads, length, length), flat32, flat, wide_flat, wide_flat, wide_flat, flat32, flat,
         shape_of(length // 2, embed), shape_of(length // 2, embed), shape_of(picks.size, embed)],
        scratch=[
            square, pltpu.VMEM((heads, 1, 2 * length), F32), pltpu.VMEM((2, 128, 2 * length), F32),
            pltpu.VMEM((2, length, length), F32), all_probs,
            pair_sems, pltpu.VMEM((length, part), F32), pltpu.VMEM((length, part), F32), pltpu.VMEM((length, embed), BF16),
        ],
        name="forward", us=25, raw_results=(5,),
    )(
        bias_table.T, Small(doc_segments), gain1, gain2, gain3, Small(picks), inputs, query_weight, key_weight,
        value_weight, output_weight, gate_weight, up_weight, down_weight, projection,
    )

    other_half = flip_stream(upper)
    both = ("stream", "wide")
    gathered = lax.all_to_all(picked.reshape(2 * width, half * top, embed), both, 0, 0, tiled=True)
    query_emb = jnp.where(is_query, lower, other_half)
    start = place * row_queries + stream * half
    losses, own_grads, pick_grads = match(
        query_emb.reshape(half, query_len, embed),
        gathered[width:].reshape(width, half, top, embed),
        lax.dynamic_slice_in_dim(query_mask, start, half, 0),
        lax.dynamic_slice_in_dim(positives, start, half, 0),
    )
    pick_grads = pick_grads.reshape(width, half * top, embed)
    returned = lax.all_to_all(
        jnp.concatenate([jnp.zeros_like(pick_grads), pick_grads], axis=0), both, 0, 0, tiled=True
    )
    loss_high = losses.astype(BF16)
    loss_low = (losses - loss_high.astype(F32)).astype(BF16)
    other_loss = flip_stream(jnp.stack([loss_high, loss_low])).astype(F32)
    other_loss = other_loss[0] + other_loss[1]
    query_loss = jnp.where(
        is_query,
        jnp.concatenate([losses, other_loss]),
        jnp.concatenate([other_loss, losses]),
    )
    own_grads = own_grads.reshape(length // 2, embed)
    other_grads = flip_stream(own_grads)

    source = blocks_ordered(jnp.arange(model, dtype=jnp.int32), width, order).reshape(1, model)
    tall = shape_of(model, length)
    n1_t, n2_t, n3_t, context_t, onehot = call(
        turn_kernel, [tall] * 4 + [shape_of(length, picks.size)], scratch=[pltpu.VMEM((model, model), BF16)], name="turn", us=4
    )(Small(source), Small(picks), normed_one, normed_two, normed_three, context)
    hidden_t = blocks_ordered(hidden.T, width, down_order)

    def core():
        return bit_of_wide(0)

    def other_core():
        return 1 - bit_of_wide(0)

    many = picks.size > 2048
    onehot_operand = Raw(onehot) if many else onehot
    pieces_of_picks = [pltpu.VMEM((length, 2048), BF16), pltpu.SemaphoreType.DMA] if many else []
    half_rows = shape_of(model // 2, hidden_width)
    (
        down_send, branch, grad_gate, grad_up, gate_send, up_send, grad_projection, grad_middle, attended,
        grad_context, shares2, shares3,
    ) = call(
        partial(upper_back_kernel, part),
        [shape_of(hidden_width // 2, model), flat, wide_flat, wide_flat, half_rows,
         half_rows, shape_of(model, embed), flat32, flat, flat, shares,
         shares],
        scratch=[
            pltpu.VMEM((length, embed), BF16), pltpu.VMEM((length, model), F32), pltpu.VMEM((length, part), F32),
            pltpu.VMEM((length, embed), F32),
        ]
        + pieces_of_picks,
        name="upper_back", us=18, after=(other_loss,), pieces={9: (0, 4), 10: (1, 4), 11: (1, 4)},
    )(
        Small(projection), gain2, gain3, own_grads, other_grads, returned.reshape(-1, embed), onehot_operand, block_out,
        Part(hidden_t, other_core, hidden_width // 2), down_weight, up_factor, gate_factor,
        Part(n2_t, other_core, model // 2), n3_t, gate_weight, up_weight, middle, output_weight,
    )
    down_recv = flip_wide(down_send, 0)
    gate_recv = flip_wide(gate_send, 0)
    up_recv = flip_wide(up_send, 0)

    down_send, down_keep = call(
        down_keep_kernel, [shape_of(hidden_width // 4, model)] * 2, name="down_keep", us=4
    )(branch, Part(hidden_t, core, hidden_width // 2), Arrived(down_recv))
    down_recv = flip_wide(down_send, 2)

    gate_send, gate_keep, up_send, up_keep = call(
        partial(gates_keep_kernel, part),
        [shape_of(model // 2, hidden_width // 2)] * 2 + [shape_of(model // 4, hidden_width)] * 2,
        name="gates_keep", us=6, after=(down_keep,),
    )(Part(n2_t, core, model // 2), grad_gate, Arrived(gate_recv), grad_up, Arrived(up_recv))
    gate_recv = flip_stream(gate_send)
    up_recv = flip_wide(up_send, 1)

    widest = 4 * model + embed
    grad_queries, grad_keys, grad_values, folded, heads_send = call(
        attend_back_kernel,
        [flat, flat, flat, shape_of(heads, 8, 2 * length, dtype=F32), shape_of(model // 2, widest)],
        scratch=[
            all_probs, pair_sems, pltpu.VMEM((2, length, length), BF16), pltpu.VMEM((2, length, length), F32),
            pltpu.VMEM((2, 128, 2 * length), F32),
        ],
        name="attend_back", us=14, after=(up_keep,),
    )(
        Small(grad_projection), Raw(probs), queries, keys, values, grad_context, Part(n1_t, other_core, model // 2),
        Part(context_t, other_core, model // 2), attended,
    )
    down_sum = halve_rows(added(down_keep, down_recv), 1)
    heads_recv = flip_wide(heads_send, 0)
    gate_sum = added(gate_keep, gate_recv)
    up_sum = added(up_keep, up_recv)
    grad_tokens, shares1 = call(
        start_back_kernel, [flat32, shares], name="start_back", us=5, after=(heads_send, down_sum, gate_recv, up_recv)
    )(gain1, grad_queries, query_weight, grad_keys, key_weight, grad_values, value_weight, inputs, grad_middle)
    a_send, a_keep, b_send, b_keep, gain_grads = call(
        heads_keep_kernel,
        [shape_of(model // 2, model)] * 2 + [shape_of(model // 4, 2 * model + embed)] * 2
        + [shape_of(3, model, dtype=F32)],
        name="heads_keep", us=4, after=(grad_tokens,),
    )(
        Small(grad_projection), Small(shares1), Small(shares2), Small(shares3), Part(n1_t, core, model // 2),
        Part(context_t, core, model // 2), grad_queries, grad_keys, grad_values, attended, heads_recv,
    )
    a_sum = added(a_keep, flip_stream(a_send))
    b_sum = added(b_keep, flip_wide(b_send, 1))

    for bit in down_order[3:]:
        down_sum = halve_rows(down_sum, bit)
    down_sum = down_sum.astype(F32) + flip_stream(down_sum).astype(F32)

    def finish(first, second):
        block = jnp.concatenate([halve_rows(first, 1), second], axis=1)
        for bit in range(2, bits):
            block = halve_rows(block, bit)
        other = flip_stream(block)
        edge = first.shape[1]
        mine, theirs = block[:, :edge].astype(F32), other[:, :edge].astype(F32)
        left, right = jnp.where(is_query, mine, theirs), jnp.where(is_query, theirs, mine)
        return left, right, block[:, edge:].astype(F32) + other[:, edge:].astype(F32)

    gate_left, gate_right, sum_up = finish(gate_sum, up_sum)
    sum_query, sum_key, rest = finish(a_sum, b_sum)
    grad_table = bias_grad_of(folded, bias_table.shape[0], length)
    small = jnp.concatenate([gain_grads.reshape(-1), grad_table.reshape(-1)])
    small = sum_everywhere(small.reshape(-1, 128), width).reshape(-1)
    own_rows = model // width
    grad_gains = [lax.dynamic_slice_in_dim(small, i * model + place * own_rows, own_rows, 0) for i in range(3)]
    return (
        query_loss,
        grad_tokens.reshape(tokens.shape),
        sum_query,
        sum_key,
        rest[:, :model],
        rest[:, model : 2 * model],
        jnp.concatenate([gate_left, gate_right], axis=1),
        sum_up,
        down_sum,
        rest[:, 2 * model :],
        grad_gains[0],
        grad_gains[1],
        grad_gains[2],
        small[3 * model :].reshape(bias_table.shape),
    )


def solution(mesh):
    rows = P("wide", None)
    in_specs = (
        P("stream", "wide", None, None),
        rows,
        P(),
        P(),
        P(None, "wide", None),
    ) + (P(),) * 12
    out_specs = (P("wide"), P("stream", "wide", None, None)) + (rows,) * 8 + (P("wide"),) * 3 + (P(),)
    return jax.shard_map(
        per_device, mesh=mesh, in_specs=in_specs, out_specs=out_specs, check_vma=False
    )
```
